128 devices in a mesh: role: 2 (over core), dev: 64 (over z, y, x).
Axes of the slice: x: 4, y: 4, z: 4, core: 2. Of those that a mesh axis runs over, the one named last changes fastest.
Arguments:
- resid: bfloat16 [512, 3584], P('dev'), may hold values from -1.5 to 1.5
- query: bfloat16 [512, 64, 576], P('dev'), may hold values from -32 to 32
- cache: bfloat16 [512, 128, 576], P('dev'), may hold values from -6 to 6
- lengths: int32 [512], P('dev'), may hold values from 2 to 128, as said below
- w_uv: bfloat16 [512, 64, 128], P(None, 'dev'), may hold values from -0.25 to 0.25
- w_out: bfloat16 [64, 128, 3584], P('dev', None, 'role'), may hold values from -0.0625 to 0.0625
- norm_gain: float32 [3584], replicated, may hold values from 0.5 to 1.5
- expert_ids: int32 [512, 8], P('dev'), may hold values from 0 to 63, as said below
- gate_scores: float32 [512, 8], P('dev'), may hold values from 0.05 to 1
- w_gate: bfloat16 [64, 3584, 1024], P('dev'), may hold values from -0.09375 to 0.09375
- w_up: bfloat16 [64, 3584, 1024], P('dev'), may hold values from -0.09375 to 0.09375
- w_down: bfloat16 [64, 1024, 3584], P('dev'), may hold values from -0.1875 to 0.1875
Outputs:
- layer_out: bfloat16 [512, 3584], P('dev', 'role')
The draws below stay inside these ranges and needn't reach their ends.
Inputs may be any that keep to these rules, and one draw needn't show every extreme that they name: `expert_ids`: within the rows of one index of dev, no expert is chosen by more than 2 rows; in the rows of the last index of dev, expert 0 is chosen by exactly 2; each row names 8 different experts. `lengths`: some sequence uses all 128 positions.
All inputs are finite; a program needn't handle non-finite values.
Results may differ from the reference program's by a relative error of at most 0.014.
Values may be sent and summed in bfloat16 or wider, within the bound.
No kernel may reach another device: no remote copies, remote signals or barrier semaphores. Data moves between devices by JAX's collectives and lax.ppermute only.
A program may use at most 128 MiB of HBM per device.

```python
import math
import jax
import jax.numpy as jnp
from jax import lax

D = 3584
FF = 1024
LAT = 512
ROPE = 64
VDIM = 128
TOP = 8
CACHE = 128
TOK_DEV = 8
HEADS = 64
EXPERTS = 64
TOKENS = 512
CAP = 2
N_DEV = 64


def latent_rows(key):
    drawn = jax.random.normal(key, (TOKENS, CACHE, LAT + ROPE), jnp.float32)
    return jnp.clip(drawn, -4.5, 4.5)


def draw_cache(key, part):
    drawn = latent_rows(key)
    return drawn.astype(jnp.bfloat16)


def draw_query(key, part):
    key = jax.random.fold_in(key, 5)
    noise = jnp.clip(jax.random.normal(key, (TOKENS, HEADS, LAT + ROPE), jnp.float32), -4.5, 4.5)
    return noise.astype(jnp.bfloat16)


def draw_lengths(key, part):
    key = jax.random.fold_in(key, 7)
    drawn = jax.random.randint(key, (TOKENS,), 2, CACHE + 1).astype(jnp.int32)
    return drawn.at[0].set(CACHE)


def draw_expert_ids(key, part):
    key = jax.random.fold_in(key, 11)
    blocks = TOKENS // TOK_DEV
    per_block = TOK_DEV * TOP
    least = per_block // CAP
    key_hot = jax.random.fold_in(key, 1)
    key_order = jax.random.fold_in(key, 2)
    key_span = jax.random.fold_in(key, 3)
    hot_count = max(1, EXPERTS // 16)
    hot_rank = jax.random.permutation(key_hot, EXPERTS).astype(jnp.int32)
    is_hot = (hot_rank < hot_count).astype(jnp.int32)
    expert_axis = jnp.arange(EXPERTS, dtype=jnp.int32)
    base = jax.random.randint(key_order, (blocks, EXPERTS), 0, 1 << 16).astype(jnp.int32)
    base = base - is_hot[None, :] * (1 << 17)
    last_block = (jnp.arange(blocks, dtype=jnp.int32) == blocks - 1)[:, None]
    first_expert = (expert_axis == 0)[None, :]
    base = jnp.where(last_block & first_expert, -(1 << 18), base)
    ranked = base * EXPERTS + expert_axis[None, :]
    order = jnp.argsort(ranked, axis=1).astype(jnp.int32)
    span = jax.random.randint(key_span, (blocks,), least, EXPERTS + 1).astype(jnp.int32)
    span = span.at[blocks - 1].set(least)
    choice_axis = jnp.arange(per_block, dtype=jnp.int32)
    position = choice_axis[None, :] % span[:, None]
    picked = jnp.take_along_axis(order, position, axis=1)
    return picked.reshape(TOKENS, TOP).astype(jnp.int32)


def block_scale(rng, extent, pieces, smallest, largest):
    factor_of, own = 1.0, jax.random.fold_in(rng, 6)
    for axis_at, parts in pieces:
        steps = jnp.exp(jax.random.uniform(jax.random.fold_in(own, axis_at), (parts,), jnp.float32, smallest / len(pieces), largest / len(pieces)))
        factor_of = factor_of * jnp.repeat(steps, extent[axis_at] // parts).reshape([-1 if axis == axis_at else 1 for axis in range(len(extent))])
    return factor_of


def scatter_about(stream_key, extent, scale, most, pieces=(), kind=jnp.bfloat16):
    values = scale * jax.random.normal(stream_key, extent, jnp.float32)
    if pieces:
        values = values * block_scale(stream_key, extent, pieces, -0.22, 0.18)
    return jnp.clip(values, -most, most).astype(kind)


def setup_inputs(seed: int = 0) -> dict:
    arg_keys = jax.random.split(jax.random.key(seed), 13)
    return {
        "resid": scatter_about(arg_keys[0], (TOKENS, D), 0.25, 1.5, ((0, 64),)),
        "query": draw_query(jax.random.fold_in(arg_keys[12], 71), 0),
        "cache": draw_cache(jax.random.fold_in(arg_keys[12], 71), 0),
        "lengths": draw_lengths(jax.random.fold_in(arg_keys[12], 71), 0),
        "w_uv": scatter_about(arg_keys[4], (LAT, HEADS, VDIM), LAT ** -0.5, 0.25, ((1, 64),)),
        "w_out": scatter_about(arg_keys[5], (HEADS, VDIM, D), (HEADS * VDIM) ** -0.5, 0.0625, ((0, 64), (2, 2))),
        "norm_gain": jnp.clip(1.0 + 0.1 * jax.random.normal(arg_keys[6], (D,), jnp.float32), 0.5, 1.5),
        "expert_ids": draw_expert_ids(jax.random.fold_in(arg_keys[12], 71), 0),
        "gate_scores": jnp.clip(jnp.exp(math.log(1.0) - 2.9957323 * jax.random.uniform(arg_keys[8], (TOKENS, TOP), jnp.float32) ** block_scale(arg_keys[8], (TOKENS, TOP), ((0, 64),), -0.2, 0.2)), 0.05, 1.0),
        "w_gate": scatter_about(arg_keys[9], (EXPERTS, D, FF), D ** -0.5, 0.09375, ((0, 64),)),
        "w_up": scatter_about(arg_keys[10], (EXPERTS, D, FF), D ** -0.5, 0.09375, ((0, 64),)),
        "w_down": scatter_about(arg_keys[11], (EXPERTS, FF, D), FF ** -0.5, 0.1875, ((0, 64),)),
    }


softmax_scale = 0.07216878364870323

def reference(resid, query, cache, lengths, w_uv, w_out, norm_gain, expert_ids, gate_scores, w_gate, w_up, w_down):
    scores = jnp.einsum('thc,tlc->thl', query.astype(jnp.float32), cache.astype(jnp.float32)) * softmax_scale
    position = jnp.arange(CACHE, dtype=jnp.int32)
    usable = position[None, None, :] < lengths[:, None, None]
    scores = jnp.where(usable, scores, -1e+30)
    row_max = lax.optimization_barrier(jnp.max(scores, axis=-1, keepdims=True))
    exponent = jnp.where(usable, jnp.exp(scores - row_max), 0.0)
    attention = (exponent / lax.optimization_barrier(jnp.sum(exponent, axis=-1, keepdims=True))).astype(jnp.bfloat16)
    context = jnp.einsum('thl,tlc->thc', attention.astype(jnp.float32), cache[:, :, :LAT].astype(jnp.float32)).astype(jnp.bfloat16)
    values = jnp.einsum('thc,chv->thv', context.astype(jnp.float32), w_uv.astype(jnp.float32)).astype(jnp.bfloat16)
    attended = jnp.dot(values.reshape(TOKENS, HEADS * VDIM), w_out.reshape(HEADS * VDIM, D), preferred_element_type=jnp.float32)
    hidden = resid.astype(jnp.float32) + attended
    normed = (hidden * lax.rsqrt(lax.optimization_barrier(jnp.mean(hidden * hidden, axis=-1, keepdims=True)) + 1e-06) * norm_gain).astype(jnp.bfloat16)
    routed = expert_ids.reshape(N_DEV, TOK_DEV * TOP)
    onehot = (routed[:, :, None] == jnp.arange(EXPERTS, dtype=jnp.int32)[None, None, :]).astype(jnp.int32)
    slot_rank = lax.optimization_barrier(jnp.sum((jnp.cumsum(onehot, axis=1) - 1) * onehot, axis=2))
    source = jnp.arange(N_DEV, dtype=jnp.int32)[:, None]
    placed = (routed * (N_DEV * CAP) + source * CAP + slot_rank).reshape(-1).astype(jnp.int32)
    token_of = (jnp.arange(TOKENS * TOP, dtype=jnp.int32) // TOP).astype(jnp.int32)
    lookup = jnp.full((EXPERTS * N_DEV * CAP,), -1, dtype=jnp.int32).at[placed].set(token_of)
    lookup = lookup.reshape(EXPERTS, N_DEV * CAP)

    def expert(operands):
        row_index, gate_mat, up_mat, down_mat = operands
        row_block = normed[jnp.maximum(row_index, 0)]
        row_block = jnp.where((row_index >= 0)[:, None], row_block, jnp.zeros_like(row_block))
        gate_part = jnp.dot(row_block, gate_mat, preferred_element_type=jnp.float32)
        up_part = jnp.dot(row_block, up_mat, preferred_element_type=jnp.float32)
        inner = (jax.nn.silu(gate_part) * up_part).astype(jnp.bfloat16)
        return jnp.dot(inner, down_mat, preferred_element_type=jnp.float32).astype(jnp.bfloat16)
    produced = lax.map(expert, (lookup, w_gate, w_up, w_down))
    picked = produced.reshape(-1, D)[placed].reshape(TOKENS, TOP, D)
    gate_weights = (2.5 * gate_scores / lax.optimization_barrier(jnp.sum(gate_scores, axis=-1, keepdims=True))).astype(jnp.bfloat16)
    combined = lax.optimization_barrier(jnp.sum(gate_weights.astype(jnp.float32)[:, :, None] * picked.astype(jnp.float32), axis=1))
    return (hidden + combined).astype(jnp.bfloat16)
```

```python
import jax
import jax.numpy as jnp
from jax import lax
from jax.sharding import PartitionSpec as P

softmax_scale = 0.07216878364870323
bf16 = jnp.bfloat16
f32 = jnp.float32


def split_terms(value):
    first = lax.reduce_precision(value, 8, 7)
    rest = value - first
    second = lax.reduce_precision(rest, 8, 7)
    third = rest - second
    return jnp.stack([first, second, third], axis=-1).astype(bf16)


def local(
    resid,
    query,
    cache,
    lengths,
    w_uv,
    w_out,
    norm_gain,
    expert_ids,
    gate_scores,
    w_gate,
    w_up,
    w_down,
):
    role_index = lax.axis_index("role")
    tok_dev, width = resid.shape
    half_width = w_out.shape[2]
    latent_width = w_uv.shape[0]
    n_dev = lax.axis_size("dev")
    top_count = expert_ids.shape[1]
    capacity = max(2, tok_dev * top_count * 2 // n_dev)
    slots = n_dev * capacity
    hidden_units = w_gate.shape[2]
    swap = [(0, 1), (1, 0)]

    scores = jnp.einsum("thc,tlc->thl", query, cache, preferred_element_type=f32) * softmax_scale
    position = jnp.arange(cache.shape[1], dtype=jnp.int32)
    usable = position[None, None, :] < lengths[:, None, None]
    scores = jnp.where(usable, scores, -1e30)
    row_max = jnp.max(scores, axis=-1, keepdims=True)
    exponent = jnp.where(usable, jnp.exp(scores - row_max), 0.0)
    attention = (exponent / jnp.sum(exponent, axis=-1, keepdims=True)).astype(bf16)
    context = jnp.einsum(
        "thl,tlc->thc", attention, cache[:, :, :latent_width], preferred_element_type=f32
    ).astype(bf16)
    by_head = lax.all_to_all(context, "dev", split_axis=1, concat_axis=0, tiled=True)
    values = jnp.dot(by_head[:, 0], w_uv[:, 0], preferred_element_type=f32).astype(bf16)
    partial = jnp.dot(values, w_out[0], preferred_element_type=f32).astype(bf16)
    pieces = lax.all_to_all(
        partial.reshape(n_dev, tok_dev, half_width), "dev", split_axis=0, concat_axis=0, tiled=True
    )
    attended = jnp.sum(pieces.astype(f32), axis=0)

    own_resid = lax.dynamic_slice_in_dim(resid, role_index * half_width, half_width, 1)
    own_gain = lax.dynamic_slice_in_dim(norm_gain, role_index * half_width, half_width, 0)
    hidden = own_resid.astype(f32) + attended
    squares = split_terms(jnp.sum(hidden * hidden, axis=-1))
    rows = jnp.concatenate(
        [(hidden * own_gain).astype(bf16), squares, jnp.zeros((tok_dev, 125), bf16)], axis=1
    )

    flat_ids = expert_ids.reshape(-1)
    onehot = (flat_ids[:, None] == jnp.arange(n_dev, dtype=jnp.int32)[None, :]).astype(jnp.int32)
    slot_rank = jnp.sum((jnp.cumsum(onehot, axis=0) - 1) * onehot, axis=1)
    placed = (flat_ids * capacity + slot_rank).reshape(tok_dev, top_count)
    slot_ids = jnp.arange(slots, dtype=jnp.int32)
    lookup = jnp.any(slot_ids[:, None, None] == placed[None, :, :], axis=-1).astype(bf16)
    packed = jnp.dot(lookup, rows, preferred_element_type=f32).astype(bf16)
    arrived = lax.all_to_all(packed, "dev", split_axis=0, concat_axis=0, tiled=True)

    row_block = arrived[:, :half_width]
    own_gate = lax.dynamic_slice_in_dim(w_gate[0], role_index * half_width, half_width, 0)
    own_up = lax.dynamic_slice_in_dim(w_up[0], role_index * half_width, half_width, 0)
    own_down = lax.dynamic_slice_in_dim(w_down[0], role_index * half_width, half_width, 1)
    gate_part = jnp.dot(row_block, own_gate, preferred_element_type=f32)
    up_part = jnp.dot(row_block, own_up, preferred_element_type=f32)
    square_terms = arrived[:, half_width:]
    outward = jnp.concatenate([gate_part.astype(bf16), up_part.astype(bf16), square_terms], axis=1)
    inward = lax.ppermute(outward, "role", swap).astype(f32)
    gate_part = gate_part + inward[:, :hidden_units]
    up_part = up_part + inward[:, hidden_units : 2 * hidden_units]
    total = jnp.sum(square_terms.astype(f32) + inward[:, 2 * hidden_units :], axis=1, keepdims=True)
    scale = lax.rsqrt(total / width + 1e-06)
    inner = (jax.nn.silu(gate_part * scale) * (up_part * scale)).astype(bf16)
    produced = jnp.dot(inner, own_down, preferred_element_type=f32).astype(bf16)
    returned = lax.all_to_all(produced, "dev", split_axis=0, concat_axis=0, tiled=True)

    gate_weights = (2.5 * gate_scores / jnp.sum(gate_scores, axis=-1, keepdims=True)).astype(bf16)
    spread = jnp.where(
        slot_ids[None, None, :] == placed[:, :, None], gate_weights.astype(f32)[:, :, None], 0.0
    )
    combine_weights = jnp.sum(spread, axis=1).astype(bf16)
    combined = jnp.dot(combine_weights, returned, preferred_element_type=f32)
    return (hidden + combined).astype(bf16)


def solution(mesh):
    return jax.shard_map(
        local,
        mesh=mesh,
        in_specs=(
            P("dev", None),
            P("dev", None, None),
            P("dev", None, None),
            P("dev"),
            P(None, "dev", None),
            P("dev", None, "role"),
            P(),
            P("dev", None),
            P("dev", None),
            P("dev", None, None),
            P("dev", None, None),
            P("dev", None, None),
        ),
        out_specs=P("dev", "role"),
        check_vma=False,
    )
```

```python
import functools

import jax
import jax.numpy as jnp
import numpy as np
from jax import lax
from jax.experimental import pallas as pl
from jax.experimental.pallas import tpu as pltpu
from jax.sharding import PartitionSpec as P

softmax_scale = 0.07216878364870323
bf16 = jnp.bfloat16
f32 = jnp.float32


def split_terms(value):
    first = lax.reduce_precision(value, 8, 7)
    rest = value - first
    second = lax.reduce_precision(rest, 8, 7)
    third = rest - second
    return jnp.stack([first, second, third], axis=-1).astype(bf16)


MIB = 1024 * 1024
in_vmem = pl.BlockSpec(memory_space=pltpu.VMEM)
in_smem = pl.BlockSpec(memory_space=pltpu.SMEM)
in_hbm = pl.BlockSpec(memory_space=pltpu.HBM)


def keep_hbm(value):
    return pltpu.with_memory_space_constraint(value, pltpu.HBM)


def visit_order(n_dev):
    return list(range(n_dev))[::-1]


def attend_kernel(
    role, lengths, query, cache, sort, sent, queries, caches, sorts, valid, staged, done
):
    heads = query.shape[1]
    block = sent.shape[1]
    run = queries.shape[1]
    latent_width = sent.shape[0] * block // (heads * 2 * run)
    chunks = latent_width // block
    loads = [
        pltpu.make_async_copy(lengths, valid, done.at[0]),
        pltpu.make_async_copy(sort, sorts, done.at[1]),
    ]
    for p in range(2):
        first = p * 2 * run + role[0] * run
        loads.append(pltpu.make_async_copy(query.at[pl.ds(first, run)], queries.at[p], done.at[2 + p]))
        loads.append(pltpu.make_async_copy(cache.at[pl.ds(first, run)], caches.at[p], done.at[4 + p]))
    for copy in loads:
        copy.start()
    for copy in loads:
        copy.wait()
    rows = run * chunks * 2
    tokens = [(p, k) for p in range(2) for k in range(run)]
    scores = [
        jnp.dot(queries[p, k], caches[p, k], preferred_element_type=f32) * softmax_scale
        for p, k in tokens
    ]
    position = lax.broadcasted_iota(jnp.int32, scores[0].shape, 1)
    usable = [position < valid[p * 2 * run + role[0] * run + k] for p, k in tokens]
    scores = [jnp.where(u, x, -1e30) for u, x in zip(usable, scores)]
    peaks = [jnp.max(x, axis=1, keepdims=True) for x in scores]
    exponents = [jnp.where(u, jnp.exp(x - m), 0.0) for u, x, m in zip(usable, scores, peaks)]
    sums = [jnp.sum(x, axis=1, keepdims=True) for x in exponents]
    attention = [(x / total).astype(bf16) for x, total in zip(exponents, sums)]
    attention = [
        jnp.dot(sorts[p], x, preferred_element_type=f32).astype(bf16)
        for (p, k), x in zip(tokens, attention)
    ]
    contexts = [
        lax.dot_general(
            x, caches[p, k, :latent_width], (((1,), (1,)), ((), ())), preferred_element_type=f32
        )
        for (p, k), x in zip(tokens, attention)
    ]
    half = heads // 2
    for (p, k), context in zip(tokens, contexts):
        for i in range(2):
            for c in range(chunks):
                at = p * rows + k * 2 * chunks + 2 * c + i
                staged[pl.ds(at, half, stride=2 * rows)] = context[
                    i * half : (i + 1) * half, c * block : (c + 1) * block
                ]
    sent[...] = staged[...].astype(bf16)


def attend(role_index, lengths, query, cache, sort, latent_width, block):
    tokens, heads, key_width = query.shape
    positions = cache.shape[1]
    run = tokens // 4
    rows = heads * run * 2 * latent_width // block
    return pl.pallas_call(
        attend_kernel,
        out_shape=jax.ShapeDtypeStruct((rows, block), bf16),
        in_specs=[in_smem] + [in_hbm] * 4,
        out_specs=in_vmem,
        scratch_shapes=[
            pltpu.VMEM((2, run, heads, key_width), bf16),
            pltpu.VMEM((2, run, key_width, positions), bf16),
            pltpu.VMEM(sort.shape, bf16),
            pltpu.SMEM((tokens,), jnp.int32),
            pltpu.VMEM((rows, block), f32),
            pltpu.SemaphoreType.DMA((6,)),
        ],
        compiler_params=pltpu.CompilerParams(vmem_limit_bytes=8 * MIB),
        name="attend",
    )(
        role_index.reshape(1),
        keep_hbm(lengths),
        keep_hbm(query),
        keep_hbm(jnp.swapaxes(cache, 1, 2)),
        keep_hbm(sort),
    )


def values_kernel(gathered, own, pair, values, staged):
    block = gathered.shape[1]
    rows = values.shape[0]
    stride = gathered.shape[0] // rows
    staged[...] = gathered[...].astype(f32)
    for i, weights in enumerate((own, pair)):
        total = jnp.zeros((rows, block), f32)
        for c in range(stride // 2):
            part = staged[pl.ds(2 * c + i, rows, stride=stride)].astype(bf16)
            total += jnp.dot(
                part, weights[c * block : (c + 1) * block], preferred_element_type=f32
            )
        values[:, i * block : (i + 1) * block] = total.astype(bf16)


def lift_values(gathered, own, pair):
    total, block = gathered.shape
    latent_width = own.shape[0]
    rows = total * block // (2 * latent_width)
    return pl.pallas_call(
        values_kernel,
        out_shape=jax.ShapeDtypeStruct((rows, 2 * block), bf16),
        in_specs=[in_vmem] * 3,
        out_specs=in_vmem,
        scratch_shapes=[pltpu.VMEM((total, block), f32)],
        compiler_params=pltpu.CompilerParams(vmem_limit_bytes=8 * MIB),
        name="lift_values",
    )(gathered, own, pair)


def project_kernel(role, own_values, other_values, own, pair, partial, spread, source):
    rows, block = own_values.shape[0], own.shape[0]
    quarter = partial.shape[1]
    run = 2
    n_dev = rows // run
    spread[...] = jnp.zeros_like(spread)
    for place, values in ((role[0], own_values), (1 - role[0], other_values)):
        for i in range(2):
            source[...] = values[:, i * block : (i + 1) * block].astype(f32)
            for k in range(run):
                part = source[pl.ds(k, n_dev, stride=run)]
                for c in range(2):
                    at = c * 2 * run + place * run + k
                    spread[2 * c + i, pl.ds(at, n_dev, stride=4 * run)] = part
    total = jnp.zeros(partial.shape, f32)
    for c in range(2):
        columns = slice(c * quarter, (c + 1) * quarter)
        left = jnp.concatenate([spread[2 * c], spread[2 * c + 1]], axis=1).astype(bf16)
        right = jnp.concatenate([own[:, columns], pair[:, columns]], axis=0)
        total += jnp.dot(left, right, preferred_element_type=f32)
    partial[...] = total.astype(bf16)


def project(role_index, own_values, other_values, own, pair):
    rows, wide = own_values.shape
    quarter = own.shape[1] // 2
    return pl.pallas_call(
        project_kernel,
        out_shape=jax.ShapeDtypeStruct((4 * rows, quarter), bf16),
        in_specs=[in_smem] + [in_vmem] * 4,
        out_specs=in_vmem,
        scratch_shapes=[
            pltpu.VMEM((4, 4 * rows, wide // 2), f32),
            pltpu.VMEM((rows, wide // 2), f32),
        ],
        compiler_params=pltpu.CompilerParams(vmem_limit_bytes=16 * MIB),
        name="project",
    )(role_index.reshape(1), own_values, other_values, own, pair)


def lift_kernel(role, arrived, gate, up, outward, own, terms, weights, done):
    blocks, step, hidden_units = weights.shape[1:]
    half = blocks * step
    start = pl.multiple_of(role[0] * half, half)
    copies = [
        [
            pltpu.make_async_copy(
                source.at[pl.ds(start + i * step, step)], weights.at[s, i], done.at[s, i]
            )
            for i in range(blocks)
        ]
        for s, source in enumerate((gate, up))
    ]
    for part in copies:
        for copy in part:
            copy.start()
    outward[:, 2 * hidden_units :] = arrived[:, half:]
    terms[...] = arrived[:, half:].astype(f32)
    for s, part in enumerate(copies):
        columns = slice(s * hidden_units, (s + 1) * hidden_units)
        for i, copy in enumerate(part):
            copy.wait()
            product = jnp.dot(
                arrived[:, i * step : (i + 1) * step], weights[s, i], preferred_element_type=f32
            )
            own[:, columns] = product if i == 0 else own[:, columns] + product
        outward[:, columns] = own[:, columns].astype(bf16)


def lift_rows(role_index, arrived, gate, up):
    half, hidden_units = gate.shape[0] // 2, gate.shape[1]
    rows, extra = arrived.shape[0], arrived.shape[1] - half
    step = 256
    blocks = half // step
    return pl.pallas_call(
        lift_kernel,
        out_shape=[
            jax.ShapeDtypeStruct((rows, 2 * hidden_units + extra), bf16),
            jax.ShapeDtypeStruct((rows, 2 * hidden_units), f32),
            jax.ShapeDtypeStruct((rows, extra), f32),
        ],
        in_specs=[in_smem, in_vmem, in_hbm, in_hbm],
        out_specs=[in_vmem] * 3,
        scratch_shapes=[
            pltpu.VMEM((2, blocks, step, hidden_units), bf16),
            pltpu.SemaphoreType.DMA((2, blocks)),
        ],
        compiler_params=pltpu.CompilerParams(vmem_limit_bytes=20 * MIB),
        name="lift_rows",
    )(role_index.reshape(1), arrived, keep_hbm(gate), keep_hbm(up))


def lower_kernel(width, role, own, inward, terms, down, produced, weights, total, done):
    blocks, step, half = weights.shape
    hidden_units = blocks * step
    copies = [
        pltpu.make_async_copy(
            down.at[pl.ds(i * step, step), pl.ds(pl.multiple_of(role[0] * half, half), half)],
            weights.at[i],
            done.at[i],
        )
        for i in range(blocks)
    ]
    for copy in copies:
        copy.start()
    squares = jnp.sum(
        terms[...] + inward[:, 2 * hidden_units :].astype(f32), axis=1, keepdims=True
    )
    scale = lax.rsqrt(squares / width + 1e-06)
    for i, copy in enumerate(copies):
        gate_at = slice(i * step, (i + 1) * step)
        up_at = slice(hidden_units + i * step, hidden_units + (i + 1) * step)
        gate_part = (own[:, gate_at] + inward[:, gate_at].astype(f32)) * scale
        up_part = (own[:, up_at] + inward[:, up_at].astype(f32)) * scale
        inner = (gate_part / (1.0 + jnp.exp(-gate_part)) * up_part).astype(bf16)
        copy.wait()
        product = jnp.dot(inner, weights[i], preferred_element_type=f32)
        total[...] = product if i == 0 else total[...] + product
    produced[...] = total[...].astype(bf16).reshape(produced.shape)


def lower_rows(role_index, width, own, inward, terms, down, capacity):
    rows, hidden_units, half = own.shape[0], down.shape[0], down.shape[1] // 2
    step = 256
    return pl.pallas_call(
        functools.partial(lower_kernel, width),
        out_shape=jax.ShapeDtypeStruct((rows, half), bf16),
        in_specs=[in_smem] + [in_vmem] * 3 + [in_hbm],
        out_specs=in_vmem,
        scratch_shapes=[
            pltpu.VMEM((hidden_units // step, step, half), bf16),
            pltpu.VMEM((rows, half), f32),
            pltpu.SemaphoreType.DMA((hidden_units // step,)),
        ],
        compiler_params=pltpu.CompilerParams(vmem_limit_bytes=16 * MIB),
        name="lower_rows",
    )(role_index.reshape(1), own, inward, terms, keep_hbm(down))


def local(
    resid,
    query,
    cache,
    lengths,
    w_uv,
    w_out,
    norm_gain,
    expert_ids,
    gate_scores,
    w_gate,
    w_up,
    w_down,
):
    role_index = lax.axis_index("role")
    tok_dev, width = resid.shape
    half_width = w_out.shape[2]
    latent_width = w_uv.shape[0]
    n_dev = lax.axis_size("dev")
    top_count = expert_ids.shape[1]
    capacity = max(2, tok_dev * top_count * 2 // n_dev)
    slots = n_dev * capacity
    swap = [(0, 1), (1, 0)]

    pairs = n_dev // 2
    quarter = half_width // 2
    order = visit_order(n_dev)
    exchange = functools.partial(
        lax.all_to_all,
        axis_name="dev",
        split_axis=0,
        concat_axis=0,
        axis_index_groups=[order],
        tiled=True,
    )
    neighbour = [(d, d ^ 1) for d in range(n_dev)]
    wanted = np.zeros((2, n_dev, n_dev), np.float32)
    for p in range(2):
        for i in range(2):
            for g in range(pairs):
                wanted[p, i * pairs + g, order[2 * g + p] ^ i] = 1.0
    own_out, own_lift = w_out[0], w_uv[:, 0]
    pair_out = lax.ppermute(own_out, "dev", neighbour)
    pair_lift = lax.ppermute(own_lift, "dev", neighbour)
    sent = attend(
        role_index,
        lengths,
        query,
        cache,
        jnp.asarray(wanted, bf16),
        latent_width,
        own_lift.shape[1],
    )
    gathered = exchange(sent.reshape(n_dev, -1, sent.shape[1]))
    gathered, pair_out, pair_lift = lax.optimization_barrier((gathered, pair_out, pair_lift))
    own_values = lift_values(gathered.reshape(sent.shape), own_lift, pair_lift)
    other_values = lax.ppermute(own_values, "role", swap)
    partial = project(role_index, own_values, other_values, own_out, pair_out)
    pieces = exchange(partial.reshape(n_dev, tok_dev, quarter))
    sums = jnp.sum(pieces.reshape(pairs, 2, tok_dev, quarter).astype(f32), axis=0)
    attended = (
        sums.reshape(2, 2, tok_dev // 2, quarter).transpose(0, 2, 1, 3).reshape(tok_dev, half_width)
    )

    own_resid = lax.dynamic_slice_in_dim(resid, role_index * half_width, half_width, 1)
    own_gain = lax.dynamic_slice_in_dim(norm_gain, role_index * half_width, half_width, 0)
    hidden = own_resid.astype(f32) + attended
    squares = split_terms(jnp.sum(hidden * hidden, axis=-1))
    rows = jnp.concatenate(
        [(hidden * own_gain).astype(bf16), squares, jnp.zeros((tok_dev, 125), bf16)], axis=1
    )

    flat_ids = expert_ids.reshape(-1)
    onehot = (flat_ids[:, None] == jnp.arange(n_dev, dtype=jnp.int32)[None, :]).astype(jnp.int32)
    slot_rank = jnp.sum((jnp.cumsum(onehot, axis=0) - 1) * onehot, axis=1)
    rank_of = np.zeros((n_dev,), np.int32)
    rank_of[order] = np.arange(n_dev, dtype=np.int32)
    expert_place = jnp.sum(onehot * jnp.asarray(rank_of)[None, :], axis=1)
    placed = (expert_place * capacity + slot_rank).reshape(tok_dev, top_count)
    slot_ids = jnp.arange(slots, dtype=jnp.int32)
    lookup = jnp.any(slot_ids[:, None, None] == placed[None, :, :], axis=-1).astype(bf16)
    packed = jnp.dot(lookup, rows, preferred_element_type=f32).astype(bf16)
    arrived = exchange(packed)

    outward, own_sums, square_terms = lift_rows(role_index, arrived, w_gate[0], w_up[0])
    inward = lax.ppermute(outward, "role", swap)
    produced = lower_rows(role_index, width, own_sums, inward, square_terms, w_down[0], capacity)
    returned = exchange(produced)

    gate_weights = (2.5 * gate_scores / jnp.sum(gate_scores, axis=-1, keepdims=True)).astype(bf16)
    spread = jnp.where(
        slot_ids[None, None, :] == placed[:, :, None], gate_weights.astype(f32)[:, :, None], 0.0
    )
    combine_weights = jnp.sum(spread, axis=1).astype(bf16)
    combined = jnp.dot(combine_weights, returned, preferred_element_type=f32)
    return (hidden + combined).astype(bf16)


def solution(mesh):
    return jax.shard_map(
        local,
        mesh=mesh,
        in_specs=(
            P("dev", None),
            P("dev", None, None),
            P("dev", None, None),
            P("dev"),
            P(None, "dev", None),
            P("dev", None, "role"),
            P(),
            P("dev", None),
            P("dev", None),
            P("dev", None, None),
            P("dev", None, None),
            P("dev", None, None),
        ),
        out_specs=P("dev", "role"),
        check_vma=False,
    )
```

```python
import functools

import jax
import jax.numpy as jnp
import numpy as np
from jax import lax
from jax.experimental import pallas as pl
from jax.experimental.pallas import tpu as pltpu
from jax.sharding import PartitionSpec as P

softmax_scale = 0.07216878364870323
bf16 = jnp.bfloat16
f32 = jnp.float32


MIB = 1024 * 1024
in_vmem = pl.BlockSpec(memory_space=pltpu.VMEM)
in_smem = pl.BlockSpec(memory_space=pltpu.SMEM)
in_hbm = pl.BlockSpec(memory_space=pltpu.HBM)


def keep_hbm(value):
    return pltpu.with_memory_space_constraint(value, pltpu.HBM)


def visit_order(n_dev):
    return list(range(n_dev))[::-1]


def attend_kernel(
    role,
    lengths,
    query,
    cache,
    sort,
    w_uv,
    w_out,
    resid,
    ids_in,
    scores_in,
    places_in,
    sent,
    own_lift,
    own_out,
    own_resid,
    taken,
    combine,
    queries,
    caches,
    sorts,
    valid,
    ids,
    gates,
    places,
    staged,
    done,
):
    half_width = own_resid.shape[1]
    start = pl.multiple_of(role[0] * half_width, half_width)
    moves = [
        pltpu.make_async_copy(ids_in, ids, done.at[6]),
        pltpu.make_async_copy(scores_in, gates, done.at[7]),
        pltpu.make_async_copy(places_in, places, done.at[8]),
        pltpu.make_async_copy(w_uv, own_lift, done.at[9]),
        pltpu.make_async_copy(w_out, own_out, done.at[10]),
        pltpu.make_async_copy(resid.at[:, pl.ds(start, half_width)], own_resid, done.at[11]),
    ]
    heads = query.shape[1]
    block = sent.shape[1]
    run = queries.shape[1]
    latent_width = sent.shape[0] * block // (heads * 2 * run)
    chunks = latent_width // block
    loads = [
        pltpu.make_async_copy(lengths, valid, done.at[0]),
        pltpu.make_async_copy(sort, sorts, done.at[1]),
    ]
    for p in range(2):
        first = p * 2 * run + role[0] * run
        loads.append(pltpu.make_async_copy(query.at[pl.ds(first, run)], queries.at[p], done.at[2 + p]))
        loads.append(pltpu.make_async_copy(cache.at[pl.ds(first, run)], caches.at[p], done.at[4 + p]))
    for copy in loads + moves:
        copy.start()
    for copy in loads:
        copy.wait()
    rows = run * chunks * 2
    tokens = [(p, k) for p in range(2) for k in range(run)]
    scores = [
        jnp.dot(queries[p, k], caches[p, k], preferred_element_type=f32) * softmax_scale
        for p, k in tokens
    ]
    position = lax.broadcasted_iota(jnp.int32, scores[0].shape, 1)
    usable = [position < valid[p * 2 * run + role[0] * run + k] for p, k in tokens]
    scores = [jnp.where(u, x, -1e30) for u, x in zip(usable, scores)]
    peaks = [jnp.max(x, axis=1, keepdims=True) for x in scores]
    exponents = [jnp.where(u, jnp.exp(x - m), 0.0) for u, x, m in zip(usable, scores, peaks)]
    sums = [jnp.sum(x, axis=1, keepdims=True) for x in exponents]
    attention = [(x / total).astype(bf16) for x, total in zip(exponents, sums)]
    attention = [
        jnp.dot(sorts[p], x, preferred_element_type=f32).astype(bf16)
        for (p, k), x in zip(tokens, attention)
    ]
    contexts = [
        lax.dot_general(
            x, caches[p, k, :latent_width], (((1,), (1,)), ((), ())), preferred_element_type=f32
        )
        for (p, k), x in zip(tokens, attention)
    ]
    half = heads // 2
    for (p, k), context in zip(tokens, contexts):
        for i in range(2):
            for c in range(chunks):
                at = p * rows + k * 2 * chunks + 2 * c + i
                staged[pl.ds(at, half, stride=2 * rows)] = context[
                    i * half : (i + 1) * half, c * block : (c + 1) * block
                ]
    sent[...] = staged[...].astype(bf16)
    for copy in moves:
        copy.wait()
    choose(ids, gates, places, taken, combine)


def choose(ids, gates, places, taken, combine):
    tokens, top_count = ids.shape
    slots = places.shape[1]
    weights = (2.5 * gates[...] / jnp.sum(gates[...], axis=1, keepdims=True)).astype(bf16)
    weights = weights.astype(f32)
    expert = jnp.broadcast_to(places[0:1], (tokens, slots))
    chosen = jnp.zeros((tokens, slots), f32)
    weight = jnp.zeros((tokens, slots), f32)
    for k in range(top_count):
        match = (ids[:, k : k + 1] == expert).astype(f32)
        chosen += match
        weight += match * weights[:, k : k + 1]
    row = lax.broadcasted_iota(jnp.int32, (tokens, slots), 0)
    rank = jnp.zeros((tokens, slots), f32)
    for t in range(tokens - 1):
        rank += jnp.where(row > t, jnp.broadcast_to(chosen[t : t + 1], (tokens, slots)), 0.0)
    held = jnp.where(rank == places[1:2].astype(f32), chosen, 0.0)
    taken[...] = held.astype(bf16)
    combine[...] = (held * weight).astype(bf16)


def attend(role_index, lengths, query, cache, sort, w_uv, w_out, resid, ids, gates, places):
    latent_width, block = w_uv.shape
    half_width = w_out.shape[1]
    slots = places.shape[1]
    tokens, heads, key_width = query.shape
    positions = cache.shape[1]
    run = tokens // 4
    rows = heads * run * 2 * latent_width // block
    return pl.pallas_call(
        attend_kernel,
        out_shape=[
            jax.ShapeDtypeStruct((rows, block), bf16),
            jax.ShapeDtypeStruct(w_uv.shape, bf16),
            jax.ShapeDtypeStruct(w_out.shape, bf16),
            jax.ShapeDtypeStruct((tokens, half_width), bf16),
            jax.ShapeDtypeStruct((tokens, slots), bf16),
            jax.ShapeDtypeStruct((tokens, slots), bf16),
        ],
        in_specs=[in_smem] + [in_hbm] * 10,
        out_specs=[in_vmem] * 6,
        scratch_shapes=[
            pltpu.VMEM((2, run, heads, key_width), bf16),
            pltpu.VMEM((2, run, key_width, positions), bf16),
            pltpu.VMEM(sort.shape, bf16),
            pltpu.SMEM((tokens,), jnp.int32),
            pltpu.VMEM(ids.shape, jnp.int32),
            pltpu.VMEM(gates.shape, f32),
            pltpu.VMEM(places.shape, jnp.int32),
            pltpu.VMEM((rows, block), f32),
            pltpu.SemaphoreType.DMA((12,)),
        ],
        compiler_params=pltpu.CompilerParams(vmem_limit_bytes=8 * MIB),
        name="attend",
    )(
        role_index.reshape(1),
        *(
            keep_hbm(value)
            for value in (
                lengths,
                query,
                jnp.swapaxes(cache, 1, 2),
                sort,
                w_uv,
                w_out,
                resid,
                ids,
                gates,
                places,
            )
        ),
    )


def values_kernel(gathered, own, pair, values, staged):
    block = gathered.shape[1]
    rows = values.shape[0]
    stride = gathered.shape[0] // rows
    staged[...] = gathered[...].astype(f32)
    for i, weights in enumerate((own, pair)):
        total = jnp.zeros((rows, block), f32)
        for c in range(stride // 2):
            part = staged[pl.ds(2 * c + i, rows, stride=stride)].astype(bf16)
            total += jnp.dot(
                part, weights[c * block : (c + 1) * block], preferred_element_type=f32
            )
        values[:, i * block : (i + 1) * block] = total.astype(bf16)


def lift_values(gathered, own, pair):
    total, block = gathered.shape
    rows = total * block // (2 * own.shape[0])
    return pl.pallas_call(
        values_kernel,
        out_shape=jax.ShapeDtypeStruct((rows, 2 * block), bf16),
        in_specs=[in_vmem] * 3,
        out_specs=in_vmem,
        scratch_shapes=[pltpu.VMEM((total, block), f32)],
        compiler_params=pltpu.CompilerParams(vmem_limit_bytes=8 * MIB),
        name="lift_values",
    )(gathered, own, pair)


def project_kernel(role, own_values, other_values, own, pair, partial, spread, source):
    rows, block = own_values.shape[0], own.shape[0]
    quarter = partial.shape[1]
    run = 2
    n_dev = rows // run
    spread[...] = jnp.zeros_like(spread)
    for place, values in ((role[0], own_values), (1 - role[0], other_values)):
        for i in range(2):
            source[...] = values[:, i * block : (i + 1) * block].astype(f32)
            for k in range(run):
                part = source[pl.ds(k, n_dev, stride=run)]
                for c in range(2):
                    at = c * 2 * run + place * run + k
                    spread[2 * c + i, pl.ds(at, n_dev, stride=4 * run)] = part
    total = jnp.zeros(partial.shape, f32)
    for c in range(2):
        columns = slice(c * quarter, (c + 1) * quarter)
        left = jnp.concatenate([spread[2 * c], spread[2 * c + 1]], axis=1).astype(bf16)
        right = jnp.concatenate([own[:, columns], pair[:, columns]], axis=0)
        total += jnp.dot(left, right, preferred_element_type=f32)
    partial[...] = total.astype(bf16)


def project(role_index, own_values, other_values, own, pair):
    rows, wide = own_values.shape
    quarter = own.shape[1] // 2
    return pl.pallas_call(
        project_kernel,
        out_shape=jax.ShapeDtypeStruct((4 * rows, quarter), bf16),
        in_specs=[in_smem] + [in_vmem] * 4,
        out_specs=in_vmem,
        scratch_shapes=[
            pltpu.VMEM((4, 4 * rows, wide // 2), f32),
            pltpu.VMEM((rows, wide // 2), f32),
        ],
        compiler_params=pltpu.CompilerParams(vmem_limit_bytes=16 * MIB),
        name="project",
    )(role_index.reshape(1), own_values, other_values, own, pair)


def settle_kernel(role, pieces, resid, gain, taken, hidden, packed, staged):
    tokens, half = hidden.shape
    quarter = pieces.shape[1]
    group = 2 * tokens
    total = jnp.zeros((group, quarter), f32)
    for g in range(pieces.shape[0] // group):
        total += pieces[g * group : (g + 1) * group].astype(f32)
    staged[...] = total
    run = tokens // 2
    for p in range(2):
        for c in range(2):
            hidden[p * run : (p + 1) * run, c * quarter : (c + 1) * quarter] = staged[
                p * tokens + c * run : p * tokens + (c + 1) * run
            ]
    own = hidden[...] + resid[...].astype(f32)
    hidden[...] = own
    square = jnp.sum(own * own, axis=1, keepdims=True)
    first = square.astype(bf16).astype(f32)
    second = (square - first).astype(bf16).astype(f32)
    third = square - first - second
    lane = lax.broadcasted_iota(jnp.int32, (tokens, packed.shape[1] - half), 1)
    terms = jnp.where(lane == 0, first, jnp.where(lane == 1, second, third))
    terms = jnp.where(lane < 3, terms, 0.0)
    rows = jnp.concatenate([own * gain[pl.ds(role[0], 1)], terms], axis=1).astype(bf16)
    packed[...] = lax.dot_general(
        taken[...], rows, (((0,), (0,)), ((), ())), preferred_element_type=f32
    ).astype(bf16)


def settle(role_index, pieces, resid, gain, taken):
    tokens, half = resid.shape
    return pl.pallas_call(
        settle_kernel,
        out_shape=[
            jax.ShapeDtypeStruct((tokens, half), f32),
            jax.ShapeDtypeStruct((taken.shape[1], half + 128), bf16),
        ],
        in_specs=[in_smem] + [in_vmem] * 4,
        out_specs=[in_vmem] * 2,
        scratch_shapes=[pltpu.VMEM((2 * tokens, pieces.shape[1]), f32)],
        compiler_params=pltpu.CompilerParams(vmem_limit_bytes=8 * MIB),
        name="settle",
    )(role_index.reshape(1), pieces, resid, gain, taken)


def lift_kernel(role, arrived, gate, up, outward, own, terms, weights, done):
    blocks, step, hidden_units = weights.shape[1:]
    half = blocks * step
    start = pl.multiple_of(role[0] * half, half)
    copies = [
        [
            pltpu.make_async_copy(
                source.at[pl.ds(start + i * step, step)], weights.at[s, i], done.at[s, i]
            )
            for i in range(blocks)
        ]
        for s, source in enumerate((gate, up))
    ]
    for part in copies:
        for copy in part:
            copy.start()
    outward[:, 2 * hidden_units :] = arrived[:, half:]
    terms[...] = arrived[:, half:].astype(f32)
    for s, part in enumerate(copies):
        columns = slice(s * hidden_units, (s + 1) * hidden_units)
        for i, copy in enumerate(part):
            copy.wait()
            product = jnp.dot(
                arrived[:, i * step : (i + 1) * step], weights[s, i], preferred_element_type=f32
            )
            own[:, columns] = product if i == 0 else own[:, columns] + product
        outward[:, columns] = own[:, columns].astype(bf16)


def lift_rows(role_index, arrived, gate, up):
    half, hidden_units = gate.shape[0] // 2, gate.shape[1]
    rows, extra = arrived.shape[0], arrived.shape[1] - half
    step = 256
    blocks = half // step
    return pl.pallas_call(
        lift_kernel,
        out_shape=[
            jax.ShapeDtypeStruct((rows, 2 * hidden_units + extra), bf16),
            jax.ShapeDtypeStruct((rows, 2 * hidden_units), f32),
            jax.ShapeDtypeStruct((rows, extra), f32),
        ],
        in_specs=[in_smem, in_vmem, in_hbm, in_hbm],
        out_specs=[in_vmem] * 3,
        scratch_shapes=[
            pltpu.VMEM((2, blocks, step, hidden_units), bf16),
            pltpu.SemaphoreType.DMA((2, blocks)),
        ],
        compiler_params=pltpu.CompilerParams(vmem_limit_bytes=20 * MIB),
        name="lift_rows",
    )(role_index.reshape(1), arrived, keep_hbm(gate), keep_hbm(up))


def lower_kernel(width, role, own, inward, terms, down, produced, weights, total, done):
    blocks, step, half = weights.shape
    hidden_units = blocks * step
    copies = [
        pltpu.make_async_copy(
            down.at[pl.ds(i * step, step), pl.ds(pl.multiple_of(role[0] * half, half), half)],
            weights.at[i],
            done.at[i],
        )
        for i in range(blocks)
    ]
    for copy in copies:
        copy.start()
    squares = jnp.sum(
        terms[...] + inward[:, 2 * hidden_units :].astype(f32), axis=1, keepdims=True
    )
    scale = lax.rsqrt(squares / width + 1e-06)
    for i, copy in enumerate(copies):
        gate_at = slice(i * step, (i + 1) * step)
        up_at = slice(hidden_units + i * step, hidden_units + (i + 1) * step)
        gate_part = (own[:, gate_at] + inward[:, gate_at].astype(f32)) * scale
        up_part = (own[:, up_at] + inward[:, up_at].astype(f32)) * scale
        inner = (gate_part / (1.0 + jnp.exp(-gate_part)) * up_part).astype(bf16)
        copy.wait()
        product = jnp.dot(inner, weights[i], preferred_element_type=f32)
        total[...] = product if i == 0 else total[...] + product
    produced[...] = total[...].astype(bf16).reshape(produced.shape)


def lower_rows(role_index, width, own, inward, terms, down, capacity):
    rows, hidden_units, half = own.shape[0], down.shape[0], down.shape[1] // 2
    step = 256
    return pl.pallas_call(
        functools.partial(lower_kernel, width),
        out_shape=jax.ShapeDtypeStruct((rows, half), bf16),
        in_specs=[in_smem] + [in_vmem] * 3 + [in_hbm],
        out_specs=in_vmem,
        scratch_shapes=[
            pltpu.VMEM((hidden_units // step, step, half), bf16),
            pltpu.VMEM((rows, half), f32),
            pltpu.SemaphoreType.DMA((hidden_units // step,)),
        ],
        compiler_params=pltpu.CompilerParams(vmem_limit_bytes=16 * MIB),
        name="lower_rows",
    )(role_index.reshape(1), own, inward, terms, keep_hbm(down))


def local(
    resid,
    query,
    cache,
    lengths,
    w_uv,
    w_out,
    norm_gain,
    expert_ids,
    gate_scores,
    w_gate,
    w_up,
    w_down,
):
    role_index = lax.axis_index("role")
    tok_dev, width = resid.shape
    half_width = w_out.shape[2]
    n_dev = lax.axis_size("dev")
    capacity = max(2, tok_dev * expert_ids.shape[1] * 2 // n_dev)
    swap = [(0, 1), (1, 0)]

    pairs = n_dev // 2
    quarter = half_width // 2
    order = visit_order(n_dev)
    exchange = functools.partial(
        lax.all_to_all,
        axis_name="dev",
        split_axis=0,
        concat_axis=0,
        axis_index_groups=[order],
        tiled=True,
    )
    neighbour = [(d, d ^ 1) for d in range(n_dev)]
    wanted = np.zeros((2, n_dev, n_dev), np.float32)
    for p in range(2):
        for i in range(2):
            for g in range(pairs):
                wanted[p, i * pairs + g, order[2 * g + p] ^ i] = 1.0
    places = np.stack([np.repeat(order, capacity), np.tile(np.arange(capacity), n_dev)])
    pair_out = lax.ppermute(w_out[0], "dev", neighbour)
    pair_lift = lax.ppermute(w_uv[:, 0], "dev", neighbour)
    sent, own_lift, own_out, own_resid, taken, combine_weights = attend(
        role_index,
        lengths,
        query,
        cache,
        jnp.asarray(wanted, bf16),
        w_uv[:, 0],
        w_out[0],
        resid,
        expert_ids,
        gate_scores,
        jnp.asarray(places, jnp.int32),
    )
    gathered = exchange(sent.reshape(n_dev, -1, sent.shape[1]))
    gathered, pair_out, pair_lift, gain = lax.optimization_barrier(
        (gathered, pair_out, pair_lift, norm_gain.reshape(2, half_width))
    )
    own_values = lift_values(gathered.reshape(sent.shape), own_lift, pair_lift)
    other_values = lax.ppermute(own_values, "role", swap)
    partial = project(role_index, own_values, other_values, own_out, pair_out)
    pieces = exchange(partial.reshape(n_dev, tok_dev, quarter))
    hidden, packed = settle(role_index, pieces.reshape(partial.shape), own_resid, gain, taken)
    arrived = exchange(packed)

    outward, own_sums, square_terms = lift_rows(role_index, arrived, w_gate[0], w_up[0])
    inward = lax.ppermute(outward, "role", swap)
    produced = lower_rows(role_index, width, own_sums, inward, square_terms, w_down[0], capacity)
    returned = exchange(produced)

    combined = jnp.dot(combine_weights, returned, preferred_element_type=f32)
    return (hidden + combined).astype(bf16)


def solution(mesh):
    return jax.shard_map(
        local,
        mesh=mesh,
        in_specs=(
            P("dev", None),
            P("dev", None, None),
            P("dev", None, None),
            P("dev"),
            P(None, "dev", None),
            P("dev", None, "role"),
            P(),
            P("dev", None),
            P("dev", None),
            P("dev", None, None),
            P("dev", None, None),
            P("dev", None, None),
        ),
        out_specs=P("dev", "role"),
        check_vma=False,
    )
```

```python
import functools

import jax
import jax.numpy as jnp
import numpy as np
from jax import lax
from jax.experimental import pallas as pl
from jax.experimental.pallas import tpu as pltpu
from jax.sharding import PartitionSpec as P

softmax_scale = 0.07216878364870323
bf16 = jnp.bfloat16
f32 = jnp.float32


MIB = 1024 * 1024
in_vmem = pl.BlockSpec(memory_space=pltpu.VMEM)
in_smem = pl.BlockSpec(memory_space=pltpu.SMEM)
in_hbm = pl.BlockSpec(memory_space=pltpu.HBM)


def keep_hbm(value):
    return pltpu.with_memory_space_constraint(value, pltpu.HBM)


flips = (0, 1, 4, 16)


def token_class(dev):
    x, y, z = dev & 1, (dev >> 2) & 1, (dev >> 4) & 1
    return 2 * (x ^ y) + (y ^ z)


def visit_order(n_dev):
    return sorted(range(n_dev), key=lambda dev: (token_class(dev), -dev))


def attend_kernel(
    role,
    lengths,
    query,
    cache,
    sort,
    w_uv,
    w_out,
    resid,
    ids_in,
    scores_in,
    places_in,
    sent,
    own_lift,
    own_out,
    own_resid,
    taken,
    combine,
    queries,
    caches,
    sorts,
    valid,
    ids,
    gates,
    places,
    staged,
    done,
):
    half_width = own_resid.shape[1]
    start = pl.multiple_of(role[0] * half_width, half_width)
    moves = [
        pltpu.make_async_copy(ids_in, ids, done.at[10]),
        pltpu.make_async_copy(scores_in, gates, done.at[11]),
        pltpu.make_async_copy(places_in, places, done.at[12]),
        pltpu.make_async_copy(w_uv, own_lift, done.at[13]),
        pltpu.make_async_copy(w_out, own_out, done.at[14]),
        pltpu.make_async_copy(resid.at[:, pl.ds(start, half_width)], own_resid, done.at[15]),
    ]
    classes, heads = queries.shape[:2]
    block = sent.shape[1]
    latent_width = sent.shape[0] * block // (classes * heads)
    chunks = latent_width // block
    loads = [
        pltpu.make_async_copy(lengths, valid, done.at[0]),
        pltpu.make_async_copy(sort, sorts, done.at[1]),
    ]
    for i in range(classes):
        token = 2 * i + role[0]
        loads.append(pltpu.make_async_copy(query.at[token], queries.at[i], done.at[2 + i]))
        loads.append(pltpu.make_async_copy(cache.at[token], caches.at[i], done.at[6 + i]))
    for copy in loads + moves:
        copy.start()
    for copy in loads:
        copy.wait()
    tokens = range(classes)
    scores = [
        jnp.dot(queries[i], caches[i], preferred_element_type=f32) * softmax_scale for i in tokens
    ]
    position = lax.broadcasted_iota(jnp.int32, scores[0].shape, 1)
    usable = [position < valid[2 * i + role[0]] for i in tokens]
    scores = [jnp.where(u, x, -1e30) for u, x in zip(usable, scores)]
    peaks = [jnp.max(x, axis=1, keepdims=True) for x in scores]
    exponents = [jnp.where(u, jnp.exp(x - m), 0.0) for u, x, m in zip(usable, scores, peaks)]
    sums = [jnp.sum(x, axis=1, keepdims=True) for x in exponents]
    attention = [(x / total).astype(bf16) for x, total in zip(exponents, sums)]
    attention = [
        jnp.dot(sorts[i], x, preferred_element_type=f32).astype(bf16)
        for i, x in zip(tokens, attention)
    ]
    contexts = [
        lax.dot_general(
            x, caches[i, :latent_width], (((1,), (1,)), ((), ())), preferred_element_type=f32
        )
        for i, x in zip(tokens, attention)
    ]
    for i, context in zip(tokens, contexts):
        for c in range(chunks):
            staged[pl.ds(i * heads * chunks + c, heads, stride=chunks)] = context[
                :, c * block : (c + 1) * block
            ]
    sent[...] = staged[...].astype(bf16)
    for copy in moves:
        copy.wait()
    choose(ids, gates, places, taken, combine)


def choose(ids, gates, places, taken, combine):
    tokens, top_count = ids.shape
    slots = places.shape[1]
    weights = (2.5 * gates[...] / jnp.sum(gates[...], axis=1, keepdims=True)).astype(bf16)
    weights = weights.astype(f32)
    expert = jnp.broadcast_to(places[0:1], (tokens, slots))
    chosen = jnp.zeros((tokens, slots), f32)
    weight = jnp.zeros((tokens, slots), f32)
    for k in range(top_count):
        match = (ids[:, k : k + 1] == expert).astype(f32)
        chosen += match
        weight += match * weights[:, k : k + 1]
    row = lax.broadcasted_iota(jnp.int32, (tokens, slots), 0)
    rank = jnp.zeros((tokens, slots), f32)
    for t in range(tokens - 1):
        rank += jnp.where(row > t, jnp.broadcast_to(chosen[t : t + 1], (tokens, slots)), 0.0)
    held = jnp.where(rank == places[1:2].astype(f32), chosen, 0.0)
    taken[...] = held.astype(bf16)
    combine[...] = (held * weight).astype(bf16)


def attend(role_index, lengths, query, cache, sort, w_uv, w_out, resid, ids, gates, places):
    latent_width, block = w_uv.shape
    half_width = w_out.shape[1]
    slots = places.shape[1]
    tokens, heads, key_width = query.shape
    positions = cache.shape[1]
    classes = len(flips)
    rows = heads * classes * latent_width // block
    return pl.pallas_call(
        attend_kernel,
        out_shape=[
            jax.ShapeDtypeStruct((rows, block), bf16),
            jax.ShapeDtypeStruct(w_uv.shape, bf16),
            jax.ShapeDtypeStruct(w_out.shape, bf16),
            jax.ShapeDtypeStruct((tokens, half_width), bf16),
            jax.ShapeDtypeStruct((tokens, slots), bf16),
            jax.ShapeDtypeStruct((tokens, slots), bf16),
        ],
        in_specs=[in_smem] + [in_hbm] * 10,
        out_specs=[in_vmem] * 6,
        scratch_shapes=[
            pltpu.VMEM((classes, heads, key_width), bf16),
            pltpu.VMEM((classes, key_width, positions), bf16),
            pltpu.VMEM(sort.shape, bf16),
            pltpu.SMEM((tokens,), jnp.int32),
            pltpu.VMEM(ids.shape, jnp.int32),
            pltpu.VMEM(gates.shape, f32),
            pltpu.VMEM(places.shape, jnp.int32),
            pltpu.VMEM((rows, block), f32),
            pltpu.SemaphoreType.DMA((16,)),
        ],
        compiler_params=pltpu.CompilerParams(vmem_limit_bytes=8 * MIB),
        name="attend",
    )(
        role_index.reshape(1),
        *(
            keep_hbm(value)
            for value in (
                lengths,
                query,
                jnp.swapaxes(cache, 1, 2),
                sort,
                w_uv,
                w_out,
                resid,
                ids,
                gates,
                places,
            )
        ),
    )


def values_kernel(gathered, own, *rest):
    *others, values, staged = rest
    block = gathered.shape[1]
    rows = values.shape[0]
    stride = gathered.shape[0] // rows
    chunks = own.shape[0] // block
    staged[...] = gathered[...].astype(f32)
    for i, weights in enumerate([own, *others]):
        total = jnp.zeros((rows, block), f32)
        for c in range(chunks):
            part = staged[pl.ds(i * chunks + c, rows, stride=stride)].astype(bf16)
            total += jnp.dot(
                part, weights[c * block : (c + 1) * block], preferred_element_type=f32
            )
        values[:, i * block : (i + 1) * block] = total.astype(bf16)


def lift_values(gathered, weights):
    total, block = gathered.shape
    wide = len(weights) * block
    rows = total * block // (len(weights) * weights[0].shape[0])
    return pl.pallas_call(
        values_kernel,
        out_shape=jax.ShapeDtypeStruct((rows, wide), bf16),
        in_specs=[in_vmem] * (1 + len(weights)),
        out_specs=in_vmem,
        scratch_shapes=[pltpu.VMEM((total, block), f32)],
        compiler_params=pltpu.CompilerParams(vmem_limit_bytes=8 * MIB),
        name="lift_values",
    )(gathered, *weights)


def project_kernel(role, own_values, other_values, *rest):
    *weights, partial, spread = rest
    rows, block = own_values.shape[0], weights[0].shape[0]
    for place, values in ((role[0], own_values), (1 - role[0], other_values)):
        for i in range(len(weights)):
            spread[i, pl.ds(place, rows, stride=2)] = values[
                :, i * block : (i + 1) * block
            ].astype(f32)
    total = jnp.zeros((2 * rows, partial.shape[2]), f32)
    for i, part in enumerate(weights):
        total += jnp.dot(spread[i].astype(bf16), part[...], preferred_element_type=f32)
    partial[...] = total.astype(bf16).reshape(partial.shape)


def project(role_index, own_values, other_values, weights):
    rows, wide = own_values.shape
    return pl.pallas_call(
        project_kernel,
        out_shape=jax.ShapeDtypeStruct((rows, 2, weights[0].shape[1]), bf16),
        in_specs=[in_smem] + [in_vmem] * (2 + len(weights)),
        out_specs=in_vmem,
        scratch_shapes=[pltpu.VMEM((len(weights), 2 * rows, wide // len(weights)), f32)],
        compiler_params=pltpu.CompilerParams(vmem_limit_bytes=16 * MIB),
        name="project",
    )(role_index.reshape(1), own_values, other_values, *weights)


def settle_kernel(role, pieces, resid, gain, taken, hidden, packed):
    tokens, half = hidden.shape
    rows = pieces.shape[0] * pieces.shape[1]
    token = lax.broadcasted_iota(jnp.int32, (tokens, rows), 0)
    row = lax.broadcasted_iota(jnp.int32, (tokens, rows), 1)
    span = 2 * rows // tokens
    ours = (row // span == token // 2) & (row % 2 == token % 2)
    attended = jnp.dot(
        ours.astype(bf16), pieces[...].reshape(rows, half), preferred_element_type=f32
    )
    own = attended + resid[...].astype(f32)
    hidden[...] = own
    square = jnp.sum(own * own, axis=1, keepdims=True)
    first = square.astype(bf16).astype(f32)
    second = (square - first).astype(bf16).astype(f32)
    third = square - first - second
    lane = lax.broadcasted_iota(jnp.int32, (tokens, packed.shape[2] - half), 1)
    terms = jnp.where(lane == 0, first, jnp.where(lane == 1, second, third))
    terms = jnp.where(lane < 3, terms, 0.0)
    sent = jnp.concatenate([own * gain[pl.ds(role[0], 1)], terms], axis=1).astype(bf16)
    packed[...] = lax.dot_general(
        taken[...], sent, (((0,), (0,)), ((), ())), preferred_element_type=f32
    ).astype(bf16).reshape(packed.shape)


def settle(role_index, pieces, resid, gain, taken, capacity):
    tokens, half = resid.shape
    return pl.pallas_call(
        settle_kernel,
        out_shape=[
            jax.ShapeDtypeStruct((tokens, half), f32),
            jax.ShapeDtypeStruct((taken.shape[1] // capacity, capacity, half + 128), bf16),
        ],
        in_specs=[in_smem] + [in_vmem] * 4,
        out_specs=[in_vmem] * 2,
        compiler_params=pltpu.CompilerParams(vmem_limit_bytes=8 * MIB),
        name="settle",
    )(role_index.reshape(1), pieces, resid, gain, taken)


def keep_vmem(value):
    return pltpu.with_memory_space_constraint(value, pltpu.VMEM)


def lift_kernel(role, arrived, gate, up, outward, own, terms, weights, done):
    blocks, step, hidden_units = weights.shape[1:]
    half = blocks * step
    start = pl.multiple_of(role[0] * half, half)
    copies = [
        [
            pltpu.make_async_copy(
                source.at[pl.ds(start + i * step, step)], weights.at[s, i], done.at[s, i]
            )
            for i in range(blocks)
        ]
        for s, source in enumerate((gate, up))
    ]
    for part in copies:
        for copy in part:
            copy.start()
    rows = arrived[...].reshape(own.shape[0], arrived.shape[2])
    outward[:, 2 * hidden_units :] = rows[:, half:]
    terms[...] = rows[:, half:].astype(f32)
    for s, part in enumerate(copies):
        columns = slice(s * hidden_units, (s + 1) * hidden_units)
        for i, copy in enumerate(part):
            copy.wait()
            product = jnp.dot(
                rows[:, i * step : (i + 1) * step], weights[s, i], preferred_element_type=f32
            )
            own[:, columns] = product if i == 0 else own[:, columns] + product
        outward[:, columns] = own[:, columns].astype(bf16)


def lift_rows(role_index, arrived, gate, up):
    half, hidden_units = gate.shape[0] // 2, gate.shape[1]
    rows, extra = arrived.shape[0] * arrived.shape[1], arrived.shape[2] - half
    step = 256
    blocks = half // step
    return pl.pallas_call(
        lift_kernel,
        out_shape=[
            jax.ShapeDtypeStruct((rows, 2 * hidden_units + extra), bf16),
            jax.ShapeDtypeStruct((rows, 2 * hidden_units), f32),
            jax.ShapeDtypeStruct((rows, extra), f32),
        ],
        in_specs=[in_smem, in_vmem, in_hbm, in_hbm],
        out_specs=[in_vmem] * 3,
        scratch_shapes=[
            pltpu.VMEM((2, blocks, step, hidden_units), bf16),
            pltpu.SemaphoreType.DMA((2, blocks)),
        ],
        compiler_params=pltpu.CompilerParams(vmem_limit_bytes=20 * MIB),
        name="lift_rows",
    )(role_index.reshape(1), arrived, keep_hbm(gate), keep_hbm(up))


def lower_kernel(width, role, own, inward, terms, down, produced):
    hidden_units, half = down.shape[0], down.shape[1] // 2
    step = 256
    squares = jnp.sum(
        terms[...] + inward[:, 2 * hidden_units :].astype(f32), axis=1, keepdims=True
    )
    scale = lax.rsqrt(squares / width + 1e-06)
    ours = pl.ds(pl.multiple_of(role[0] * half, 128), half)
    total = jnp.zeros((own.shape[0], half), f32)
    for i in range(hidden_units // step):
        gate_at = slice(i * step, (i + 1) * step)
        up_at = slice(hidden_units + i * step, hidden_units + (i + 1) * step)
        gate_part = (own[:, gate_at] + inward[:, gate_at].astype(f32)) * scale
        up_part = (own[:, up_at] + inward[:, up_at].astype(f32)) * scale
        inner = (gate_part / (1.0 + jnp.exp(-gate_part)) * up_part).astype(bf16)
        total += jnp.dot(inner, down[gate_at, ours], preferred_element_type=f32)
    produced[...] = total.astype(bf16).reshape(produced.shape)


def lower_rows(role_index, width, own, inward, terms, down, capacity):
    rows, half = own.shape[0], down.shape[1] // 2
    return pl.pallas_call(
        functools.partial(lower_kernel, width),
        out_shape=jax.ShapeDtypeStruct((rows // capacity, capacity, half), bf16),
        in_specs=[in_smem] + [in_vmem] * 4,
        out_specs=in_vmem,
        compiler_params=pltpu.CompilerParams(vmem_limit_bytes=8 * MIB),
        name="lower_rows",
    )(role_index.reshape(1), own, inward, terms, keep_vmem(down))


def combine_kernel(weights, returned, hidden, out):
    rows = returned.shape[0] * returned.shape[1]
    combined = jnp.dot(
        weights[...], returned[...].reshape(rows, out.shape[1]), preferred_element_type=f32
    )
    out[...] = (hidden[...] + combined).astype(bf16)


def combine(weights, returned, hidden):
    return pl.pallas_call(
        combine_kernel,
        out_shape=jax.ShapeDtypeStruct(hidden.shape, bf16),
        in_specs=[in_vmem] * 3,
        out_specs=in_vmem,
        compiler_params=pltpu.CompilerParams(vmem_limit_bytes=8 * MIB),
        name="combine",
    )(weights, returned, hidden)


def local(
    resid,
    query,
    cache,
    lengths,
    w_uv,
    w_out,
    norm_gain,
    expert_ids,
    gate_scores,
    w_gate,
    w_up,
    w_down,
):
    role_index = lax.axis_index("role")
    tok_dev, width = resid.shape
    half_width = w_out.shape[2]
    n_dev = lax.axis_size("dev")
    capacity = max(2, tok_dev * expert_ids.shape[1] * 2 // n_dev)
    swap = [(0, 1), (1, 0)]

    order = visit_order(n_dev)
    exchange = functools.partial(
        lax.all_to_all,
        axis_name="dev",
        split_axis=0,
        concat_axis=0,
        axis_index_groups=[order],
        tiled=True,
    )
    span = n_dev // len(flips)
    wanted = np.zeros((len(flips), n_dev, n_dev), np.float32)
    for place, dev in enumerate(order):
        for i, flip in enumerate(flips):
            wanted[place // span, place % span * len(flips) + i, dev ^ flip] = 1.0
    places = np.stack([np.repeat(order, capacity), np.tile(np.arange(capacity), n_dev)])
    steps = [[(dev, dev ^ flip) for dev in range(n_dev)] for flip in flips[1:]]
    other_outs = [lax.ppermute(w_out[0], "dev", step) for step in steps]
    sent, own_lift, own_out, own_resid, taken, combine_weights = attend(
        role_index,
        lengths,
        query,
        cache,
        jnp.asarray(wanted, bf16),
        w_uv[:, 0],
        w_out[0],
        resid,
        expert_ids,
        gate_scores,
        jnp.asarray(places, jnp.int32),
    )
    other_lifts = [lax.ppermute(own_lift, "dev", step) for step in steps]
    gathered = exchange(sent.reshape(n_dev, -1, sent.shape[1]))
    gathered, other_outs, other_lifts, gain = lax.optimization_barrier(
        (gathered, other_outs, other_lifts, norm_gain.reshape(2, half_width))
    )
    own_values = lift_values(gathered.reshape(sent.shape), [own_lift, *other_lifts])
    other_values = lax.ppermute(own_values, "role", swap)
    partial = project(role_index, own_values, other_values, [own_out, *other_outs])
    pieces = exchange(partial)
    hidden, packed = settle(role_index, pieces, own_resid, gain, taken, capacity)
    arrived = exchange(packed)

    outward, own_sums, square_terms = lift_rows(role_index, arrived, w_gate[0], w_up[0])
    inward = lax.ppermute(outward, "role", swap)
    produced = lower_rows(role_index, width, own_sums, inward, square_terms, w_down[0], capacity)
    returned = exchange(produced)

    return combine(combine_weights, returned, hidden)


def solution(mesh):
    return jax.shard_map(
        local,
        mesh=mesh,
        in_specs=(
            P("dev", None),
            P("dev", None, None),
            P("dev", None, None),
            P("dev"),
            P(None, "dev", None),
            P("dev", None, "role"),
            P(),
            P("dev", None),
            P("dev", None),
            P("dev", None, None),
            P("dev", None, None),
            P("dev", None, None),
        ),
        out_specs=P("dev", "role"),
        check_vma=False,
    )
```

```python
import functools

import jax
import jax.numpy as jnp
import numpy as np
from jax import lax
from jax.experimental import pallas as pl
from jax.experimental.pallas import tpu as pltpu
from jax.sharding import PartitionSpec as P

softmax_scale = 0.07216878364870323
bf16 = jnp.bfloat16
f32 = jnp.float32


MIB = 1024 * 1024
in_vmem = pl.BlockSpec(memory_space=pltpu.VMEM)
in_smem = pl.BlockSpec(memory_space=pltpu.SMEM)
in_hbm = pl.BlockSpec(memory_space=pltpu.HBM)


def keep_hbm(value):
    return pltpu.with_memory_space_constraint(value, pltpu.HBM)


flips = (0, 1, 4, 16)


def token_class(dev):
    x, y, z = dev & 1, (dev >> 2) & 1, (dev >> 4) & 1
    return 2 * (x ^ y) + (y ^ z)


def visit_order(n_dev):
    return sorted(range(n_dev), key=lambda dev: (-token_class(dev), -dev))


def attend_kernel(
    role,
    lengths,
    query,
    cache,
    sort,
    w_uv,
    w_out,
    resid,
    ids_in,
    scores_in,
    places_in,
    sent,
    own_lift,
    own_out,
    own_resid,
    taken,
    combine,
    queries,
    caches,
    sorts,
    valid,
    ids,
    gates,
    places,
    staged,
    done,
):
    half_width = own_resid.shape[1]
    start = pl.multiple_of(role[0] * half_width, half_width)
    moves = [
        pltpu.make_async_copy(ids_in, ids, done.at[10]),
        pltpu.make_async_copy(scores_in, gates, done.at[11]),
        pltpu.make_async_copy(places_in, places, done.at[12]),
        pltpu.make_async_copy(w_uv, own_lift, done.at[13]),
        pltpu.make_async_copy(w_out, own_out, done.at[14]),
        pltpu.make_async_copy(resid.at[:, pl.ds(start, half_width)], own_resid, done.at[15]),
    ]
    classes, heads = queries.shape[:2]
    block = sent.shape[1]
    latent_width = sent.shape[0] * block // (classes * heads)
    chunks = latent_width // block
    loads = [
        pltpu.make_async_copy(lengths, valid, done.at[0]),
        pltpu.make_async_copy(sort, sorts, done.at[1]),
    ]
    for i in range(classes):
        token = 2 * i + role[0]
        loads.append(pltpu.make_async_copy(query.at[token], queries.at[i], done.at[2 + i]))
        loads.append(pltpu.make_async_copy(cache.at[token], caches.at[i], done.at[6 + i]))
    for copy in loads + moves:
        copy.start()
    for copy in loads:
        copy.wait()
    tokens = range(classes)
    scores = [
        jnp.dot(queries[i], caches[i], preferred_element_type=f32) * softmax_scale for i in tokens
    ]
    position = lax.broadcasted_iota(jnp.int32, scores[0].shape, 1)
    usable = [position < valid[2 * i + role[0]] for i in tokens]
    scores = [jnp.where(u, x, -1e30) for u, x in zip(usable, scores)]
    peaks = [jnp.max(x, axis=1, keepdims=True) for x in scores]
    exponents = [jnp.where(u, jnp.exp(x - m), 0.0) for u, x, m in zip(usable, scores, peaks)]
    sums = [jnp.sum(x, axis=1, keepdims=True) for x in exponents]
    attention = [(x / total).astype(bf16) for x, total in zip(exponents, sums)]
    attention = [
        jnp.dot(sorts[i], x, preferred_element_type=f32).astype(bf16)
        for i, x in zip(tokens, attention)
    ]
    contexts = [
        lax.dot_general(
            x, caches[i, :latent_width], (((1,), (1,)), ((), ())), preferred_element_type=f32
        )
        for i, x in zip(tokens, attention)
    ]
    for i, context in zip(tokens, contexts):
        for c in range(chunks):
            staged[pl.ds(i * heads * chunks + c, heads, stride=chunks)] = context[
                :, c * block : (c + 1) * block
            ]
    sent[...] = staged[...].astype(bf16)
    for copy in moves:
        copy.wait()
    choose(ids, gates, places, taken, combine)


def choose(ids, gates, places, taken, combine):
    tokens, top_count = ids.shape
    slots = places.shape[1]
    weights = (2.5 * gates[...] / jnp.sum(gates[...], axis=1, keepdims=True)).astype(bf16)
    weights = weights.astype(f32)
    expert = jnp.broadcast_to(places[0:1], (tokens, slots))
    chosen = jnp.zeros((tokens, slots), f32)
    weight = jnp.zeros((tokens, slots), f32)
    for k in range(top_count):
        match = (ids[:, k : k + 1] == expert).astype(f32)
        chosen += match
        weight += match * weights[:, k : k + 1]
    row = lax.broadcasted_iota(jnp.int32, (tokens, slots), 0)
    rank = jnp.zeros((tokens, slots), f32)
    for t in range(tokens - 1):
        rank += jnp.where(row > t, jnp.broadcast_to(chosen[t : t + 1], (tokens, slots)), 0.0)
    held = jnp.where(rank == places[1:2].astype(f32), chosen, 0.0)
    taken[...] = held.astype(bf16)
    combine[...] = (held * weight).astype(bf16)


def attend(role_index, lengths, query, cache, sort, w_uv, w_out, resid, ids, gates, places):
    latent_width, block = w_uv.shape
    half_width = w_out.shape[1]
    slots = places.shape[1]
    tokens, heads, key_width = query.shape
    positions = cache.shape[1]
    classes = len(flips)
    rows = heads * classes * latent_width // block
    return pl.pallas_call(
        attend_kernel,
        out_shape=[
            jax.ShapeDtypeStruct((rows, block), bf16),
            jax.ShapeDtypeStruct(w_uv.shape, bf16),
            jax.ShapeDtypeStruct(w_out.shape, bf16),
            jax.ShapeDtypeStruct((tokens, half_width), bf16),
            jax.ShapeDtypeStruct((tokens, slots), bf16),
            jax.ShapeDtypeStruct((tokens, slots), bf16),
        ],
        in_specs=[in_smem] + [in_hbm] * 10,
        out_specs=[in_vmem] * 6,
        scratch_shapes=[
            pltpu.VMEM((classes, heads, key_width), bf16),
            pltpu.VMEM((classes, key_width, positions), bf16),
            pltpu.VMEM(sort.shape, bf16),
            pltpu.SMEM((tokens,), jnp.int32),
            pltpu.VMEM(ids.shape, jnp.int32),
            pltpu.VMEM(gates.shape, f32),
            pltpu.VMEM(places.shape, jnp.int32),
            pltpu.VMEM((rows, block), f32),
            pltpu.SemaphoreType.DMA((16,)),
        ],
        compiler_params=pltpu.CompilerParams(vmem_limit_bytes=8 * MIB),
        name="attend",
    )(
        role_index.reshape(1),
        *(
            keep_hbm(value)
            for value in (
                lengths,
                query,
                jnp.swapaxes(cache, 1, 2),
                sort,
                w_uv,
                w_out,
                resid,
                ids,
                gates,
                places,
            )
        ),
    )


def values_kernel(gathered, own, *rest):
    *others, values, staged = rest
    block = gathered.shape[1]
    rows = values.shape[0]
    stride = gathered.shape[0] // rows
    chunks = own.shape[0] // block
    staged[...] = gathered[...].astype(f32)
    for i, weights in enumerate([own, *others]):
        total = jnp.zeros((rows, block), f32)
        for c in range(chunks):
            part = staged[pl.ds(i * chunks + c, rows, stride=stride)].astype(bf16)
            total += jnp.dot(
                part, weights[c * block : (c + 1) * block], preferred_element_type=f32
            )
        values[:, i * block : (i + 1) * block] = total.astype(bf16)


def lift_values(gathered, weights):
    total, block = gathered.shape
    wide = len(weights) * block
    rows = total * block // (len(weights) * weights[0].shape[0])
    return pl.pallas_call(
        values_kernel,
        out_shape=jax.ShapeDtypeStruct((rows, wide), bf16),
        in_specs=[in_vmem] * (1 + len(weights)),
        out_specs=in_vmem,
        scratch_shapes=[pltpu.VMEM((total, block), f32)],
        compiler_params=pltpu.CompilerParams(vmem_limit_bytes=8 * MIB),
        name="lift_values",
    )(gathered, *weights)


def project_kernel(role, own_values, other_values, *rest):
    *weights, partial, spread = rest
    rows, block = own_values.shape[0], weights[0].shape[0]
    for place, values in ((role[0], own_values), (1 - role[0], other_values)):
        for i in range(len(weights)):
            spread[i, pl.ds(place, rows, stride=2)] = values[
                :, i * block : (i + 1) * block
            ].astype(f32)
    total = jnp.zeros((2 * rows, partial.shape[2]), f32)
    for i, part in enumerate(weights):
        total += jnp.dot(spread[i].astype(bf16), part[...], preferred_element_type=f32)
    partial[...] = total.astype(bf16).reshape(partial.shape)


def project(role_index, own_values, other_values, weights):
    rows, wide = own_values.shape
    return pl.pallas_call(
        project_kernel,
        out_shape=jax.ShapeDtypeStruct((rows, 2, weights[0].shape[1]), bf16),
        in_specs=[in_smem] + [in_vmem] * (2 + len(weights)),
        out_specs=in_vmem,
        scratch_shapes=[pltpu.VMEM((len(weights), 2 * rows, wide // len(weights)), f32)],
        compiler_params=pltpu.CompilerParams(vmem_limit_bytes=16 * MIB),
        name="project",
    )(role_index.reshape(1), own_values, other_values, *weights)


def settle_kernel(pieces, resid, taken, hidden, packed):
    tokens, half = hidden.shape
    rows = pieces.shape[0] * pieces.shape[1]
    token = lax.broadcasted_iota(jnp.int32, (tokens, rows), 0)
    row = lax.broadcasted_iota(jnp.int32, (tokens, rows), 1)
    span = 2 * rows // tokens
    ours = (row // span == token // 2) & (row % 2 == token % 2)
    attended = jnp.dot(
        ours.astype(bf16), pieces[...].reshape(rows, half), preferred_element_type=f32
    )
    own = attended + resid[...].astype(f32)
    hidden[...] = own
    packed[...] = lax.dot_general(
        taken[...], own.astype(bf16), (((0,), (0,)), ((), ())), preferred_element_type=f32
    ).astype(bf16).reshape(packed.shape)


def settle(pieces, resid, taken, capacity):
    tokens, half = resid.shape
    return pl.pallas_call(
        settle_kernel,
        out_shape=[
            jax.ShapeDtypeStruct((tokens, half), f32),
            jax.ShapeDtypeStruct((taken.shape[1] // capacity, capacity, half), bf16),
        ],
        in_specs=[in_vmem] * 3,
        out_specs=[in_vmem] * 2,
        compiler_params=pltpu.CompilerParams(vmem_limit_bytes=8 * MIB),
        name="settle",
    )(pieces, resid, taken)


def keep_vmem(value):
    return pltpu.with_memory_space_constraint(value, pltpu.VMEM)


def lift_kernel(role, arrived, gain, gate, up, outward, own, terms, weights, done):
    blocks, step, hidden_units = weights.shape[1:]
    half = blocks * step
    start = pl.multiple_of(role[0] * half, half)
    copies = [
        [
            pltpu.make_async_copy(
                source.at[pl.ds(start + i * step, step)], weights.at[s, i], done.at[s, i]
            )
            for i in range(blocks)
        ]
        for s, source in enumerate((gate, up))
    ]
    for part in copies:
        for copy in part:
            copy.start()
    rows = arrived[...].reshape(own.shape[0], half).astype(f32)
    square = jnp.sum(rows * rows, axis=1, keepdims=True)
    first = square.astype(bf16).astype(f32)
    second = (square - first).astype(bf16).astype(f32)
    third = square - first - second
    lane = lax.broadcasted_iota(jnp.int32, terms.shape, 1)
    split = jnp.where(lane == 0, first, jnp.where(lane == 1, second, third))
    split = jnp.where(lane < 3, split, 0.0)
    terms[...] = split
    outward[:, 2 * hidden_units :] = split.astype(bf16)
    rows = (rows * gain[pl.ds(role[0], 1)]).astype(bf16)
    for s, part in enumerate(copies):
        columns = slice(s * hidden_units, (s + 1) * hidden_units)
        for i, copy in enumerate(part):
            copy.wait()
            product = jnp.dot(
                rows[:, i * step : (i + 1) * step], weights[s, i], preferred_element_type=f32
            )
            own[:, columns] = product if i == 0 else own[:, columns] + product
        outward[:, columns] = own[:, columns].astype(bf16)


def lift_rows(role_index, arrived, gain, gate, up):
    half, hidden_units = gate.shape[0] // 2, gate.shape[1]
    rows, extra = arrived.shape[0] * arrived.shape[1], 128
    step = 256
    blocks = half // step
    return pl.pallas_call(
        lift_kernel,
        out_shape=[
            jax.ShapeDtypeStruct((rows, 2 * hidden_units + extra), bf16),
            jax.ShapeDtypeStruct((rows, 2 * hidden_units), f32),
            jax.ShapeDtypeStruct((rows, extra), f32),
        ],
        in_specs=[in_smem, in_vmem, in_vmem, in_hbm, in_hbm],
        out_specs=[in_vmem] * 3,
        scratch_shapes=[
            pltpu.VMEM((2, blocks, step, hidden_units), bf16),
            pltpu.SemaphoreType.DMA((2, blocks)),
        ],
        compiler_params=pltpu.CompilerParams(vmem_limit_bytes=20 * MIB),
        name="lift_rows",
    )(role_index.reshape(1), arrived, gain, keep_hbm(gate), keep_hbm(up))


def lower_kernel(width, role, own, inward, terms, down, produced):
    hidden_units, half = down.shape[0], down.shape[1] // 2
    step = 256
    squares = jnp.sum(
        terms[...] + inward[:, 2 * hidden_units :].astype(f32), axis=1, keepdims=True
    )
    scale = lax.rsqrt(squares / width + 1e-06)
    ours = pl.ds(pl.multiple_of(role[0] * half, 128), half)
    total = jnp.zeros((own.shape[0], half), f32)
    for i in range(hidden_units // step):
        gate_at = slice(i * step, (i + 1) * step)
        up_at = slice(hidden_units + i * step, hidden_units + (i + 1) * step)
        gate_part = (own[:, gate_at] + inward[:, gate_at].astype(f32)) * scale
        up_part = (own[:, up_at] + inward[:, up_at].astype(f32)) * scale
        inner = (gate_part / (1.0 + jnp.exp(-gate_part)) * up_part).astype(bf16)
        total += jnp.dot(inner, down[gate_at, ours], preferred_element_type=f32)
    produced[...] = total.astype(bf16).reshape(produced.shape)


def lower_rows(role_index, width, own, inward, terms, down, capacity):
    rows, half = own.shape[0], down.shape[1] // 2
    return pl.pallas_call(
        functools.partial(lower_kernel, width),
        out_shape=jax.ShapeDtypeStruct((rows // capacity, capacity, half), bf16),
        in_specs=[in_smem] + [in_vmem] * 4,
        out_specs=in_vmem,
        compiler_params=pltpu.CompilerParams(vmem_limit_bytes=8 * MIB),
        name="lower_rows",
    )(role_index.reshape(1), own, inward, terms, keep_vmem(down))


def combine_kernel(weights, returned, hidden, out):
    rows = returned.shape[0] * returned.shape[1]
    combined = jnp.dot(
        weights[...], returned[...].reshape(rows, out.shape[1]), preferred_element_type=f32
    )
    out[...] = (hidden[...] + combined).astype(bf16)


def combine(weights, returned, hidden):
    return pl.pallas_call(
        combine_kernel,
        out_shape=jax.ShapeDtypeStruct(hidden.shape, bf16),
        in_specs=[in_vmem] * 3,
        out_specs=in_vmem,
        compiler_params=pltpu.CompilerParams(vmem_limit_bytes=8 * MIB),
        name="combine",
    )(weights, returned, hidden)


def local(
    resid,
    query,
    cache,
    lengths,
    w_uv,
    w_out,
    norm_gain,
    expert_ids,
    gate_scores,
    w_gate,
    w_up,
    w_down,
):
    role_index = lax.axis_index("role")
    tok_dev, width = resid.shape
    half_width = w_out.shape[2]
    n_dev = lax.axis_size("dev")
    capacity = max(2, tok_dev * expert_ids.shape[1] * 2 // n_dev)
    swap = [(0, 1), (1, 0)]

    order = visit_order(n_dev)
    exchange = functools.partial(
        lax.all_to_all,
        axis_name="dev",
        split_axis=0,
        concat_axis=0,
        axis_index_groups=[order],
        tiled=True,
    )
    span = n_dev // len(flips)
    wanted = np.zeros((len(flips), n_dev, n_dev), np.float32)
    for place, dev in enumerate(order):
        for i, flip in enumerate(flips):
            wanted[place // span, place % span * len(flips) + i, dev ^ flip] = 1.0
    places = np.stack([np.repeat(order, capacity), np.tile(np.arange(capacity), n_dev)])
    steps = [[(dev, dev ^ flip) for dev in range(n_dev)] for flip in flips[1:]]
    other_outs = [lax.ppermute(w_out[0], "dev", step) for step in steps]
    sent, own_lift, own_out, own_resid, taken, combine_weights = attend(
        role_index,
        lengths,
        query,
        cache,
        jnp.asarray(wanted, bf16),
        w_uv[:, 0],
        w_out[0],
        resid,
        expert_ids,
        gate_scores,
        jnp.asarray(places, jnp.int32),
    )
    other_lifts = [lax.ppermute(own_lift, "dev", step) for step in steps]
    gathered = exchange(sent.reshape(n_dev, -1, sent.shape[1]))
    gathered, other_outs, other_lifts, gain = lax.optimization_barrier(
        (gathered, other_outs, other_lifts, norm_gain.reshape(2, half_width))
    )
    own_values = lift_values(gathered.reshape(sent.shape), [own_lift, *other_lifts])
    other_values = lax.ppermute(own_values, "role", swap)
    partial = project(role_index, own_values, other_values, [own_out, *other_outs])
    pieces = exchange(partial)
    hidden, packed = settle(pieces, own_resid, taken, capacity)
    arrived = exchange(packed)

    outward, own_sums, square_terms = lift_rows(role_index, arrived, gain, w_gate[0], w_up[0])
    inward = lax.ppermute(outward, "role", swap)
    produced = lower_rows(role_index, width, own_sums, inward, square_terms, w_down[0], capacity)
    returned = exchange(produced)

    return combine(combine_weights, returned, hidden)


def solution(mesh):
    return jax.shard_map(
        local,
        mesh=mesh,
        in_specs=(
            P("dev", None),
            P("dev", None, None),
            P("dev", None, None),
            P("dev"),
            P(None, "dev", None),
            P("dev", None, "role"),
            P(),
            P("dev", None),
            P("dev", None),
            P("dev", None, None),
            P("dev", None, None),
            P("dev", None, None),
        ),
        out_specs=P("dev", "role"),
        check_vma=False,
    )
```

```python
import functools

import jax
import jax.numpy as jnp
import numpy as np
from jax import lax
from jax.experimental import pallas as pl
from jax.experimental.pallas import tpu as pltpu
from jax.sharding import PartitionSpec as P

softmax_scale = 0.07216878364870323
bf16 = jnp.bfloat16
f32 = jnp.float32


MIB = 1024 * 1024
in_vmem = pl.BlockSpec(memory_space=pltpu.VMEM)
in_smem = pl.BlockSpec(memory_space=pltpu.SMEM)
in_hbm = pl.BlockSpec(memory_space=pltpu.HBM)


def keep_hbm(value):
    return pltpu.with_memory_space_constraint(value, pltpu.HBM)


flips = (0, 1, 4, 16)


def token_class(dev):
    x, y, z = dev & 1, (dev >> 2) & 1, (dev >> 4) & 1
    return 2 * (x ^ y) + (y ^ z)


def visit_order(n_dev):
    return sorted(range(n_dev), key=lambda dev: (-token_class(dev), -dev))


def attend_kernel(
    role,
    lengths,
    query,
    cache,
    sort,
    w_uv,
    w_out,
    resid,
    ids_in,
    scores_in,
    places_in,
    sent,
    own_lift,
    own_out,
    own_resid,
    taken,
    combine,
    queries,
    caches,
    sorts,
    valid,
    ids,
    gates,
    places,
    staged,
    done,
):
    half_width = own_resid.shape[1]
    start = pl.multiple_of(role[0] * half_width, half_width)
    moves = [
        pltpu.make_async_copy(ids_in, ids, done.at[10]),
        pltpu.make_async_copy(scores_in, gates, done.at[11]),
        pltpu.make_async_copy(places_in, places, done.at[12]),
        pltpu.make_async_copy(w_uv, own_lift, done.at[13]),
        pltpu.make_async_copy(w_out, own_out, done.at[14]),
        pltpu.make_async_copy(resid.at[:, pl.ds(start, half_width)], own_resid, done.at[15]),
    ]
    classes, heads = queries.shape[:2]
    block = sent.shape[1]
    latent_width = sent.shape[0] * block // (classes * heads)
    chunks = latent_width // block
    loads = [
        pltpu.make_async_copy(lengths, valid, done.at[0]),
        pltpu.make_async_copy(sort, sorts, done.at[1]),
    ]
    for i in range(classes):
        token = 2 * i + role[0]
        loads.append(pltpu.make_async_copy(query.at[token], queries.at[i], done.at[2 + i]))
        loads.append(pltpu.make_async_copy(cache.at[token], caches.at[i], done.at[6 + i]))
    for copy in loads + moves:
        copy.start()
    for copy in loads:
        copy.wait()
    tokens = range(classes)
    scores = [
        jnp.dot(queries[i], caches[i], preferred_element_type=f32) * softmax_scale for i in tokens
    ]
    position = lax.broadcasted_iota(jnp.int32, scores[0].shape, 1)
    usable = [position < valid[2 * i + role[0]] for i in tokens]
    scores = [jnp.where(u, x, -1e30) for u, x in zip(usable, scores)]
    peaks = [jnp.max(x, axis=1, keepdims=True) for x in scores]
    exponents = [jnp.where(u, jnp.exp(x - m), 0.0) for u, x, m in zip(usable, scores, peaks)]
    sums = [jnp.sum(x, axis=1, keepdims=True) for x in exponents]
    attention = [(x / total).astype(bf16) for x, total in zip(exponents, sums)]
    attention = [
        jnp.dot(sorts[i], x, preferred_element_type=f32).astype(bf16)
        for i, x in zip(tokens, attention)
    ]
    contexts = [
        lax.dot_general(
            x, caches[i, :latent_width], (((1,), (1,)), ((), ())), preferred_element_type=f32
        )
        for i, x in zip(tokens, attention)
    ]
    for i, context in zip(tokens, contexts):
        for c in range(chunks):
            staged[pl.ds(i * heads * chunks + c, heads, stride=chunks)] = context[
                :, c * block : (c + 1) * block
            ]
    sent[...] = staged[: sent.shape[0]].astype(bf16)
    for copy in moves:
        copy.wait()
    choose(ids, gates, places, taken, combine)


def choose(ids, gates, places, taken, combine):
    tokens, top_count = ids.shape
    slots = places.shape[1]
    weights = (2.5 * gates[...] / jnp.sum(gates[...], axis=1, keepdims=True)).astype(bf16)
    weights = weights.astype(f32)
    expert = jnp.broadcast_to(places[0:1], (tokens, slots))
    chosen = jnp.zeros((tokens, slots), f32)
    weight = jnp.zeros((tokens, slots), f32)
    for k in range(top_count):
        match = (ids[:, k : k + 1] == expert).astype(f32)
        chosen += match
        weight += match * weights[:, k : k + 1]
    row = lax.broadcasted_iota(jnp.int32, (tokens, slots), 0)
    rank = jnp.zeros((tokens, slots), f32)
    for t in range(tokens - 1):
        rank += jnp.where(row > t, jnp.broadcast_to(chosen[t : t + 1], (tokens, slots)), 0.0)
    held = jnp.where(rank == places[1:2].astype(f32), chosen, 0.0)
    taken[...] = held.astype(bf16)
    combine[...] = (held * weight).astype(bf16)


def attend(role_index, lengths, query, cache, sort, w_uv, w_out, resid, ids, gates, places):
    latent_width, block = w_uv.shape
    half_width = w_out.shape[1]
    slots = places.shape[1]
    tokens, heads, key_width = query.shape
    positions = cache.shape[1]
    classes = len(flips)
    rows = heads * classes * latent_width // block
    return pl.pallas_call(
        attend_kernel,
        out_shape=[
            jax.ShapeDtypeStruct((rows, block), bf16),
            jax.ShapeDtypeStruct(w_uv.shape, bf16),
            jax.ShapeDtypeStruct(w_out.shape, bf16),
            jax.ShapeDtypeStruct((tokens, half_width), bf16),
            jax.ShapeDtypeStruct((tokens, slots), bf16),
            jax.ShapeDtypeStruct((tokens, slots), bf16),
        ],
        in_specs=[in_smem] + [in_hbm] * 10,
        out_specs=[in_vmem] * 6,
        scratch_shapes=[
            pltpu.VMEM((classes, heads, key_width), bf16),
            pltpu.VMEM((classes, key_width, positions), bf16),
            pltpu.VMEM(sort.shape, bf16),
            pltpu.SMEM((tokens,), jnp.int32),
            pltpu.VMEM(ids.shape, jnp.int32),
            pltpu.VMEM(gates.shape, f32),
            pltpu.VMEM(places.shape, jnp.int32),
            pltpu.VMEM((rows + 32, block), f32),
            pltpu.SemaphoreType.DMA((16,)),
        ],
        compiler_params=pltpu.CompilerParams(vmem_limit_bytes=8 * MIB),
        name="attend",
    )(
        role_index.reshape(1),
        *(
            keep_hbm(value)
            for value in (
                lengths,
                query,
                jnp.swapaxes(cache, 1, 2),
                sort,
                w_uv,
                w_out,
                resid,
                ids,
                gates,
                places,
            )
        ),
    )


def values_kernel(gathered, own, *rest):
    *others, values, staged = rest
    block = gathered.shape[1]
    rows = values.shape[0]
    stride = gathered.shape[0] // rows
    chunks = own.shape[0] // block
    staged[: gathered.shape[0]] = gathered[...].astype(f32)
    for i, weights in enumerate([own, *others]):
        total = jnp.zeros((rows, block), f32)
        for c in range(chunks):
            part = staged[pl.ds(i * chunks + c, rows, stride=stride)].astype(bf16)
            total += jnp.dot(
                part, weights[c * block : (c + 1) * block], preferred_element_type=f32
            )
        values[:, i * block : (i + 1) * block] = total.astype(bf16)


def lift_values(gathered, weights):
    total, block = gathered.shape
    wide = len(weights) * block
    rows = total * block // (len(weights) * weights[0].shape[0])
    return pl.pallas_call(
        values_kernel,
        out_shape=jax.ShapeDtypeStruct((rows, wide), bf16),
        in_specs=[in_vmem] * (1 + len(weights)),
        out_specs=in_vmem,
        scratch_shapes=[pltpu.VMEM((total + 32, block), f32)],
        compiler_params=pltpu.CompilerParams(vmem_limit_bytes=8 * MIB),
        name="lift_values",
    )(gathered, *weights)


def project_kernel(role, own_values, other_values, *rest):
    *weights, partial, spread = rest
    rows, block = own_values.shape[0], weights[0].shape[0]
    for place, values in ((role[0], own_values), (1 - role[0], other_values)):
        for i in range(len(weights)):
            spread[i, pl.ds(place, rows, stride=2)] = values[
                :, i * block : (i + 1) * block
            ].astype(f32)
    total = jnp.zeros((2 * rows, partial.shape[2]), f32)
    for i, part in enumerate(weights):
        total += jnp.dot(spread[i, : 2 * rows].astype(bf16), part[...], preferred_element_type=f32)
    partial[...] = total.astype(bf16).reshape(partial.shape)


def project(role_index, own_values, other_values, weights):
    rows, wide = own_values.shape
    return pl.pallas_call(
        project_kernel,
        out_shape=jax.ShapeDtypeStruct((rows, 2, weights[0].shape[1]), bf16),
        in_specs=[in_smem] + [in_vmem] * (2 + len(weights)),
        out_specs=in_vmem,
        scratch_shapes=[pltpu.VMEM((len(weights), 2 * rows + 16, wide // len(weights)), f32)],
        compiler_params=pltpu.CompilerParams(vmem_limit_bytes=16 * MIB),
        name="project",
    )(role_index.reshape(1), own_values, other_values, *weights)


def settle_kernel(pieces, resid, taken, hidden, packed):
    tokens, half = hidden.shape
    rows = pieces.shape[0] * pieces.shape[1]
    token = lax.broadcasted_iota(jnp.int32, (tokens, rows), 0)
    row = lax.broadcasted_iota(jnp.int32, (tokens, rows), 1)
    span = 2 * rows // tokens
    ours = (row // span == token // 2) & (row % 2 == token % 2)
    attended = jnp.dot(
        ours.astype(bf16), pieces[...].reshape(rows, half), preferred_element_type=f32
    )
    own = attended + resid[...].astype(f32)
    hidden[...] = own
    packed[...] = lax.dot_general(
        taken[...], own.astype(bf16), (((0,), (0,)), ((), ())), preferred_element_type=f32
    ).astype(bf16).reshape(packed.shape)


def settle(pieces, resid, taken, capacity):
    tokens, half = resid.shape
    return pl.pallas_call(
        settle_kernel,
        out_shape=[
            jax.ShapeDtypeStruct((tokens, half), f32),
            jax.ShapeDtypeStruct((taken.shape[1] // capacity, capacity, half), bf16),
        ],
        in_specs=[in_vmem] * 3,
        out_specs=[in_vmem] * 2,
        compiler_params=pltpu.CompilerParams(vmem_limit_bytes=8 * MIB),
        name="settle",
    )(pieces, resid, taken)


def keep_vmem(value):
    return pltpu.with_memory_space_constraint(value, pltpu.VMEM)


def lift_kernel(role, arrived, gain, gate, up, outward, own, terms, weights, done):
    blocks, step, hidden_units = weights.shape[1:]
    half = blocks * step
    start = pl.multiple_of(role[0] * half, half)
    copies = [
        [
            pltpu.make_async_copy(
                source.at[pl.ds(start + i * step, step)], weights.at[s, i], done.at[s, i]
            )
            for i in range(blocks)
        ]
        for s, source in enumerate((gate, up))
    ]
    for part in copies:
        for copy in part:
            copy.start()
    rows = arrived[...].reshape(own.shape[0], half).astype(f32)
    square = jnp.sum(rows * rows, axis=1, keepdims=True)
    first = square.astype(bf16).astype(f32)
    second = (square - first).astype(bf16).astype(f32)
    third = square - first - second
    lane = lax.broadcasted_iota(jnp.int32, terms.shape, 1)
    split = jnp.where(lane == 0, first, jnp.where(lane == 1, second, third))
    split = jnp.where(lane < 3, split, 0.0)
    terms[...] = split
    outward[:, 2 * hidden_units :] = split.astype(bf16)
    rows = (rows * gain[pl.ds(role[0], 1)]).astype(bf16)
    for s, part in enumerate(copies):
        columns = slice(s * hidden_units, (s + 1) * hidden_units)
        for i, copy in enumerate(part):
            copy.wait()
            product = jnp.dot(
                rows[:, i * step : (i + 1) * step], weights[s, i], preferred_element_type=f32
            )
            own[:, columns] = product if i == 0 else own[:, columns] + product
        outward[:, columns] = own[:, columns].astype(bf16)


def lift_rows(role_index, arrived, gain, gate, up):
    half, hidden_units = gate.shape[0] // 2, gate.shape[1]
    rows, extra = arrived.shape[0] * arrived.shape[1], 128
    step = 256
    blocks = half // step
    return pl.pallas_call(
        lift_kernel,
        out_shape=[
            jax.ShapeDtypeStruct((rows, 2 * hidden_units + extra), bf16),
            jax.ShapeDtypeStruct((rows, 2 * hidden_units), f32),
            jax.ShapeDtypeStruct((rows, extra), f32),
        ],
        in_specs=[in_smem, in_vmem, in_vmem, in_hbm, in_hbm],
        out_specs=[in_vmem] * 3,
        scratch_shapes=[
            pltpu.VMEM((2, blocks, step, hidden_units), bf16),
            pltpu.SemaphoreType.DMA((2, blocks)),
        ],
        compiler_params=pltpu.CompilerParams(vmem_limit_bytes=20 * MIB),
        name="lift_rows",
    )(role_index.reshape(1), arrived, gain, keep_hbm(gate), keep_hbm(up))


def lower_kernel(width, role, own, inward, terms, down, produced):
    hidden_units, half = down.shape[0], down.shape[1] // 2
    step = 256
    squares = jnp.sum(
        terms[...] + inward[:, 2 * hidden_units :].astype(f32), axis=1, keepdims=True
    )
    scale = lax.rsqrt(squares / width + 1e-06)
    ours = pl.ds(pl.multiple_of(role[0] * half, 128), half)
    total = jnp.zeros((own.shape[0], half), f32)
    for i in range(hidden_units // step):
        gate_at = slice(i * step, (i + 1) * step)
        up_at = slice(hidden_units + i * step, hidden_units + (i + 1) * step)
        gate_part = (own[:, gate_at] + inward[:, gate_at].astype(f32)) * scale
        up_part = (own[:, up_at] + inward[:, up_at].astype(f32)) * scale
        inner = (gate_part / (1.0 + jnp.exp(-gate_part)) * up_part).astype(bf16)
        total += jnp.dot(inner, down[gate_at, ours], preferred_element_type=f32)
    produced[...] = total.astype(bf16).reshape(produced.shape)


def lower_rows(role_index, width, own, inward, terms, down, capacity):
    rows, half = own.shape[0], down.shape[1] // 2
    return pl.pallas_call(
        functools.partial(lower_kernel, width),
        out_shape=jax.ShapeDtypeStruct((rows // capacity, capacity, half), bf16),
        in_specs=[in_smem] + [in_vmem] * 4,
        out_specs=in_vmem,
        compiler_params=pltpu.CompilerParams(vmem_limit_bytes=8 * MIB),
        name="lower_rows",
    )(role_index.reshape(1), own, inward, terms, keep_vmem(down))


def combine_kernel(weights, returned, hidden, out):
    rows = returned.shape[0] * returned.shape[1]
    combined = jnp.dot(
        weights[...], returned[...].reshape(rows, out.shape[1]), preferred_element_type=f32
    )
    out[...] = (hidden[...] + combined).astype(bf16)


def combine(weights, returned, hidden):
    return pl.pallas_call(
        combine_kernel,
        out_shape=jax.ShapeDtypeStruct(hidden.shape, bf16),
        in_specs=[in_vmem] * 3,
        out_specs=in_vmem,
        compiler_params=pltpu.CompilerParams(vmem_limit_bytes=8 * MIB),
        name="combine",
    )(weights, returned, hidden)


def local(
    resid,
    query,
    cache,
    lengths,
    w_uv,
    w_out,
    norm_gain,
    expert_ids,
    gate_scores,
    w_gate,
    w_up,
    w_down,
):
    role_index = lax.axis_index("role")
    tok_dev, width = resid.shape
    half_width = w_out.shape[2]
    n_dev = lax.axis_size("dev")
    capacity = max(2, tok_dev * expert_ids.shape[1] * 2 // n_dev)
    swap = [(0, 1), (1, 0)]

    order = visit_order(n_dev)
    exchange = functools.partial(
        lax.all_to_all,
        axis_name="dev",
        split_axis=0,
        concat_axis=0,
        axis_index_groups=[order],
        tiled=True,
    )
    span = n_dev // len(flips)
    wanted = np.zeros((len(flips), n_dev, n_dev), np.float32)
    for place, dev in enumerate(order):
        for i, flip in enumerate(flips):
            wanted[place // span, place % span * len(flips) + i, dev ^ flip] = 1.0
    places = np.stack([np.repeat(order, capacity), np.tile(np.arange(capacity), n_dev)])
    steps = [[(dev, dev ^ flip) for dev in range(n_dev)] for flip in flips[1:]]
    other_outs = [lax.ppermute(w_out[0], "dev", step) for step in steps]
    sent, own_lift, own_out, own_resid, taken, combine_weights = attend(
        role_index,
        lengths,
        query,
        cache,
        jnp.asarray(wanted, bf16),
        w_uv[:, 0],
        w_out[0],
        resid,
        expert_ids,
        gate_scores,
        jnp.asarray(places, jnp.int32),
    )
    other_lifts = [lax.ppermute(own_lift, "dev", step) for step in steps]
    gathered = exchange(sent.reshape(n_dev, -1, sent.shape[1]))
    gathered, other_outs, other_lifts, gain = lax.optimization_barrier(
        (gathered, other_outs, other_lifts, norm_gain.reshape(2, half_width))
    )
    own_values = lift_values(gathered.reshape(sent.shape), [own_lift, *other_lifts])
    other_values = lax.ppermute(own_values, "role", swap)
    partial = project(role_index, own_values, other_values, [own_out, *other_outs])
    pieces = exchange(partial)
    hidden, packed = settle(pieces, own_resid, taken, capacity)
    arrived = exchange(packed)

    outward, own_sums, square_terms = lift_rows(role_index, arrived, gain, w_gate[0], w_up[0])
    inward = lax.ppermute(outward, "role", swap)
    produced = lower_rows(role_index, width, own_sums, inward, square_terms, w_down[0], capacity)
    returned = exchange(produced)

    return combine(combine_weights, returned, hidden)


def solution(mesh):
    return jax.shard_map(
        local,
        mesh=mesh,
        in_specs=(
            P("dev", None),
            P("dev", None, None),
            P("dev", None, None),
            P("dev"),
            P(None, "dev", None),
            P("dev", None, "role"),
            P(),
            P("dev", None),
            P("dev", None),
            P("dev", None, None),
            P("dev", None, None),
            P("dev", None, None),
        ),
        out_specs=P("dev", "role"),
        check_vma=False,
    )
```

```python
import functools

import jax
import jax.numpy as jnp
import numpy as np
from jax import lax
from jax.experimental import pallas as pl
from jax.experimental.pallas import tpu as pltpu
from jax.sharding import PartitionSpec as P

softmax_scale = 0.07216878364870323
bf16 = jnp.bfloat16
f32 = jnp.float32


MIB = 1024 * 1024
in_vmem = pl.BlockSpec(memory_space=pltpu.VMEM)
in_smem = pl.BlockSpec(memory_space=pltpu.SMEM)
in_hbm = pl.BlockSpec(memory_space=pltpu.HBM)


def keep_hbm(value):
    return pltpu.with_memory_space_constraint(value, pltpu.HBM)


flips = (0, 1, 4, 16)


def token_class(dev):
    x, y, z = dev & 1, (dev >> 2) & 1, (dev >> 4) & 1
    return 2 * (x ^ y) + (y ^ z)


def visit_order(n_dev):
    return sorted(range(n_dev), key=lambda dev: (-token_class(dev), -dev))


def attend_kernel(
    role,
    lengths,
    query,
    cache,
    sort,
    w_uv,
    w_out,
    resid,
    ids_in,
    scores_in,
    places_in,
    sent,
    own_lift,
    own_out,
    own_resid,
    taken,
    combine,
    queries,
    caches,
    sorts,
    valid,
    ids,
    gates,
    places,
    staged,
    done,
):
    half_width = own_resid.shape[1]
    start = pl.multiple_of(role[0] * half_width, half_width)
    moves = [
        pltpu.make_async_copy(ids_in, ids, done.at[10]),
        pltpu.make_async_copy(scores_in, gates, done.at[11]),
        pltpu.make_async_copy(places_in.at[role[0]], places, done.at[12]),
        pltpu.make_async_copy(w_uv, own_lift, done.at[13]),
        pltpu.make_async_copy(w_out, own_out, done.at[14]),
        pltpu.make_async_copy(resid.at[:, pl.ds(start, half_width)], own_resid, done.at[15]),
    ]
    classes, heads = queries.shape[:2]
    block = sent.shape[1]
    latent_width = sent.shape[0] * block // (classes * heads)
    chunks = latent_width // block
    loads = [
        pltpu.make_async_copy(lengths, valid, done.at[0]),
        pltpu.make_async_copy(sort.at[role[0]], sorts, done.at[1]),
    ]
    for i in range(classes):
        token = 2 * lax.rem(i + classes // 2 * role[0], classes) + role[0]
        loads.append(pltpu.make_async_copy(query.at[token], queries.at[i], done.at[2 + i]))
        loads.append(pltpu.make_async_copy(cache.at[token], caches.at[i], done.at[6 + i]))
    for copy in loads + moves:
        copy.start()
    for copy in loads:
        copy.wait()
    tokens = range(classes)
    scores = [
        jnp.dot(queries[i], caches[i], preferred_element_type=f32) * softmax_scale for i in tokens
    ]
    position = lax.broadcasted_iota(jnp.int32, scores[0].shape, 1)
    usable = [
        position < valid[2 * lax.rem(i + classes // 2 * role[0], classes) + role[0]] for i in tokens
    ]
    scores = [jnp.where(u, x, -1e30) for u, x in zip(usable, scores)]
    peaks = [jnp.max(x, axis=1, keepdims=True) for x in scores]
    exponents = [jnp.where(u, jnp.exp(x - m), 0.0) for u, x, m in zip(usable, scores, peaks)]
    sums = [jnp.sum(x, axis=1, keepdims=True) for x in exponents]
    attention = [(x / total).astype(bf16) for x, total in zip(exponents, sums)]
    attention = [
        jnp.dot(sorts[i], x, preferred_element_type=f32).astype(bf16)
        for i, x in zip(tokens, attention)
    ]
    contexts = [
        lax.dot_general(
            x, caches[i, :latent_width], (((1,), (1,)), ((), ())), preferred_element_type=f32
        )
        for i, x in zip(tokens, attention)
    ]
    for i, context in zip(tokens, contexts):
        for c in range(chunks):
            staged[pl.ds(i * heads * chunks + c, heads, stride=chunks)] = context[
                :, c * block : (c + 1) * block
            ]
    sent[...] = staged[: sent.shape[0]].astype(bf16)
    for copy in moves:
        copy.wait()
    choose(ids, gates, places, taken, combine)


def choose(ids, gates, places, taken, combine):
    tokens, top_count = ids.shape
    slots = places.shape[1]
    weights = (2.5 * gates[...] / jnp.sum(gates[...], axis=1, keepdims=True)).astype(bf16)
    weights = weights.astype(f32)
    expert = jnp.broadcast_to(places[0:1], (tokens, slots))
    chosen = jnp.zeros((tokens, slots), f32)
    weight = jnp.zeros((tokens, slots), f32)
    for k in range(top_count):
        match = (ids[:, k : k + 1] == expert).astype(f32)
        chosen += match
        weight += match * weights[:, k : k + 1]
    row = lax.broadcasted_iota(jnp.int32, (tokens, slots), 0)
    rank = jnp.zeros((tokens, slots), f32)
    for t in range(tokens - 1):
        rank += jnp.where(row > t, jnp.broadcast_to(chosen[t : t + 1], (tokens, slots)), 0.0)
    held = jnp.where(rank == places[1:2].astype(f32), chosen, 0.0)
    taken[...] = held.astype(bf16)
    combine[...] = (held * weight).astype(bf16)


def attend(role_index, lengths, query, cache, sort, w_uv, w_out, resid, ids, gates, places):
    latent_width, block = w_uv.shape
    half_width = w_out.shape[1]
    slots = places.shape[2]
    tokens, heads, key_width = query.shape
    positions = cache.shape[1]
    classes = len(flips)
    rows = heads * classes * latent_width // block
    return pl.pallas_call(
        attend_kernel,
        out_shape=[
            jax.ShapeDtypeStruct((rows, block), bf16),
            jax.ShapeDtypeStruct(w_uv.shape, bf16),
            jax.ShapeDtypeStruct(w_out.shape, bf16),
            jax.ShapeDtypeStruct((tokens, half_width), bf16),
            jax.ShapeDtypeStruct((tokens, slots), bf16),
            jax.ShapeDtypeStruct((tokens, slots), bf16),
        ],
        in_specs=[in_smem] + [in_hbm] * 10,
        out_specs=[in_vmem] * 6,
        scratch_shapes=[
            pltpu.VMEM((classes, heads, key_width), bf16),
            pltpu.VMEM((classes, key_width, positions), bf16),
            pltpu.VMEM(sort.shape[1:], bf16),
            pltpu.SMEM((tokens,), jnp.int32),
            pltpu.VMEM(ids.shape, jnp.int32),
            pltpu.VMEM(gates.shape, f32),
            pltpu.VMEM(places.shape[1:], jnp.int32),
            pltpu.VMEM((rows + 32, block), f32),
            pltpu.SemaphoreType.DMA((16,)),
        ],
        compiler_params=pltpu.CompilerParams(vmem_limit_bytes=8 * MIB),
        name="attend",
    )(
        role_index.reshape(1),
        *(
            keep_hbm(value)
            for value in (
                lengths,
                query,
                jnp.swapaxes(cache, 1, 2),
                sort,
                w_uv,
                w_out,
                resid,
                ids,
                gates,
                places,
            )
        ),
    )


def values_kernel(gathered, own, *rest):
    *others, values, staged = rest
    block = gathered.shape[1]
    rows = values.shape[0]
    stride = gathered.shape[0] // rows
    chunks = own.shape[0] // block
    staged[: gathered.shape[0]] = gathered[...].astype(f32)
    for i, weights in enumerate([own, *others]):
        total = jnp.zeros((rows, block), f32)
        for c in range(chunks):
            part = staged[pl.ds(i * chunks + c, rows, stride=stride)].astype(bf16)
            total += jnp.dot(
                part, weights[c * block : (c + 1) * block], preferred_element_type=f32
            )
        values[:, i * block : (i + 1) * block] = total.astype(bf16)


def lift_values(gathered, weights):
    total, block = gathered.shape
    wide = len(weights) * block
    rows = total * block // (len(weights) * weights[0].shape[0])
    return pl.pallas_call(
        values_kernel,
        out_shape=jax.ShapeDtypeStruct((rows, wide), bf16),
        in_specs=[in_vmem] * (1 + len(weights)),
        out_specs=in_vmem,
        scratch_shapes=[pltpu.VMEM((total + 32, block), f32)],
        compiler_params=pltpu.CompilerParams(vmem_limit_bytes=8 * MIB),
        name="lift_values",
    )(gathered, *weights)


def turned(value):
    half = value.shape[0] // 2
    return jnp.concatenate([value[half:], value[:half]], axis=0)


def project_kernel(role, own_values, other_values, *rest):
    *weights, partial, spread = rest
    rows, block = own_values.shape[0], weights[0].shape[0]
    for place, values in ((role[0], own_values[...]), (1 - role[0], turned(other_values[...]))):
        for i in range(len(weights)):
            spread[i, pl.ds(place, rows, stride=2)] = values[
                :, i * block : (i + 1) * block
            ].astype(f32)
    total = jnp.zeros((2 * rows, partial.shape[2]), f32)
    for i, part in enumerate(weights):
        total += jnp.dot(spread[i, : 2 * rows].astype(bf16), part[...], preferred_element_type=f32)
    partial[...] = total.astype(bf16).reshape(partial.shape)


def project(role_index, own_values, other_values, weights):
    rows, wide = own_values.shape
    return pl.pallas_call(
        project_kernel,
        out_shape=jax.ShapeDtypeStruct((rows, 2, weights[0].shape[1]), bf16),
        in_specs=[in_smem] + [in_vmem] * (2 + len(weights)),
        out_specs=in_vmem,
        scratch_shapes=[pltpu.VMEM((len(weights), 2 * rows + 16, wide // len(weights)), f32)],
        compiler_params=pltpu.CompilerParams(vmem_limit_bytes=16 * MIB),
        name="project",
    )(role_index.reshape(1), own_values, other_values, *weights)


def settle_kernel(role, pieces, resid, taken, hidden, packed):
    tokens, half = hidden.shape
    rows = pieces.shape[0] * pieces.shape[1]
    token = lax.broadcasted_iota(jnp.int32, (tokens, rows), 0)
    row = lax.broadcasted_iota(jnp.int32, (tokens, rows), 1)
    span = 2 * rows // tokens
    source = (row // span + tokens // 4 * role[0]) % (tokens // 2)
    ours = (source == token // 2) & (row % 2 == token % 2)
    attended = jnp.dot(
        ours.astype(bf16), pieces[...].reshape(rows, half), preferred_element_type=f32
    )
    own = attended + resid[...].astype(f32)
    hidden[...] = own
    packed[...] = lax.dot_general(
        taken[...], own.astype(bf16), (((0,), (0,)), ((), ())), preferred_element_type=f32
    ).astype(bf16).reshape(packed.shape)


def settle(role_index, pieces, resid, taken, capacity):
    tokens, half = resid.shape
    return pl.pallas_call(
        settle_kernel,
        out_shape=[
            jax.ShapeDtypeStruct((tokens, half), f32),
            jax.ShapeDtypeStruct((taken.shape[1] // capacity, capacity, half), bf16),
        ],
        in_specs=[in_smem] + [in_vmem] * 3,
        out_specs=[in_vmem] * 2,
        compiler_params=pltpu.CompilerParams(vmem_limit_bytes=8 * MIB),
        name="settle",
    )(role_index.reshape(1), pieces, resid, taken)


def keep_vmem(value):
    return pltpu.with_memory_space_constraint(value, pltpu.VMEM)


def lift_kernel(role, arrived, gain, gate, up, outward, own, terms, weights, done):
    blocks, step, hidden_units = weights.shape[1:]
    half = blocks * step
    start = pl.multiple_of(role[0] * half, half)
    copies = [
        [
            pltpu.make_async_copy(
                source.at[pl.ds(start + i * step, step)], weights.at[s, i], done.at[s, i]
            )
            for i in range(blocks)
        ]
        for s, source in enumerate((gate, up))
    ]
    for part in copies:
        for copy in part:
            copy.start()
    rows = arrived[...].reshape(own.shape[0], half).astype(f32)
    square = jnp.sum(rows * rows, axis=1, keepdims=True)
    first = square.astype(bf16).astype(f32)
    second = (square - first).astype(bf16).astype(f32)
    third = square - first - second
    lane = lax.broadcasted_iota(jnp.int32, terms.shape, 1)
    split = jnp.where(lane == 0, first, jnp.where(lane == 1, second, third))
    split = jnp.where(lane < 3, split, 0.0)
    terms[...] = split
    outward[:, 2 * hidden_units :] = split.astype(bf16)
    rows = (rows * gain[pl.ds(role[0], 1)]).astype(bf16)
    for s, part in enumerate(copies):
        columns = slice(s * hidden_units, (s + 1) * hidden_units)
        for i, copy in enumerate(part):
            copy.wait()
            product = jnp.dot(
                rows[:, i * step : (i + 1) * step], weights[s, i], preferred_element_type=f32
            )
            own[:, columns] = product if i == 0 else own[:, columns] + product
        outward[:, columns] = own[:, columns].astype(bf16)


def lift_rows(role_index, arrived, gain, gate, up):
    half, hidden_units = gate.shape[0] // 2, gate.shape[1]
    rows, extra = arrived.shape[0] * arrived.shape[1], 128
    step = 256
    blocks = half // step
    return pl.pallas_call(
        lift_kernel,
        out_shape=[
            jax.ShapeDtypeStruct((rows, 2 * hidden_units + extra), bf16),
            jax.ShapeDtypeStruct((rows, 2 * hidden_units), f32),
            jax.ShapeDtypeStruct((rows, extra), f32),
        ],
        in_specs=[in_smem, in_vmem, in_vmem, in_hbm, in_hbm],
        out_specs=[in_vmem] * 3,
        scratch_shapes=[
            pltpu.VMEM((2, blocks, step, hidden_units), bf16),
            pltpu.SemaphoreType.DMA((2, blocks)),
        ],
        compiler_params=pltpu.CompilerParams(vmem_limit_bytes=20 * MIB),
        name="lift_rows",
    )(role_index.reshape(1), arrived, gain, keep_hbm(gate), keep_hbm(up))


def lower_kernel(width, role, own, inward, terms, down, produced):
    hidden_units, half = down.shape[0], down.shape[1] // 2
    step = 256
    squares = jnp.sum(
        terms[...] + turned(inward[:, 2 * hidden_units :]).astype(f32), axis=1, keepdims=True
    )
    scale = lax.rsqrt(squares / width + 1e-06)
    ours = pl.ds(pl.multiple_of(role[0] * half, 128), half)
    total = jnp.zeros((own.shape[0], half), f32)
    for i in range(hidden_units // step):
        gate_at = slice(i * step, (i + 1) * step)
        up_at = slice(hidden_units + i * step, hidden_units + (i + 1) * step)
        gate_part = (own[:, gate_at] + turned(inward[:, gate_at]).astype(f32)) * scale
        up_part = (own[:, up_at] + turned(inward[:, up_at]).astype(f32)) * scale
        inner = (gate_part / (1.0 + jnp.exp(-gate_part)) * up_part).astype(bf16)
        total += jnp.dot(inner, down[gate_at, ours], preferred_element_type=f32)
    produced[...] = total.astype(bf16).reshape(produced.shape)


def lower_rows(role_index, width, own, inward, terms, down, capacity):
    rows, half = own.shape[0], down.shape[1] // 2
    return pl.pallas_call(
        functools.partial(lower_kernel, width),
        out_shape=jax.ShapeDtypeStruct((rows // capacity, capacity, half), bf16),
        in_specs=[in_smem] + [in_vmem] * 4,
        out_specs=in_vmem,
        compiler_params=pltpu.CompilerParams(vmem_limit_bytes=8 * MIB),
        name="lower_rows",
    )(role_index.reshape(1), own, inward, terms, keep_vmem(down))


def combine_kernel(weights, returned, hidden, out):
    rows = returned.shape[0] * returned.shape[1]
    combined = jnp.dot(
        weights[...], returned[...].reshape(rows, out.shape[1]), preferred_element_type=f32
    )
    out[...] = (hidden[...] + combined).astype(bf16)


def combine(weights, returned, hidden):
    return pl.pallas_call(
        combine_kernel,
        out_shape=jax.ShapeDtypeStruct(hidden.shape, bf16),
        in_specs=[in_vmem] * 3,
        out_specs=in_vmem,
        compiler_params=pltpu.CompilerParams(vmem_limit_bytes=8 * MIB),
        name="combine",
    )(weights, returned, hidden)


def local(
    resid,
    query,
    cache,
    lengths,
    w_uv,
    w_out,
    norm_gain,
    expert_ids,
    gate_scores,
    w_gate,
    w_up,
    w_down,
):
    role_index = lax.axis_index("role")
    tok_dev, width = resid.shape
    half_width = w_out.shape[2]
    n_dev = lax.axis_size("dev")
    capacity = max(2, tok_dev * expert_ids.shape[1] * 2 // n_dev)
    swap = [(0, 1), (1, 0)]

    order = visit_order(n_dev)
    orders = [order, order[n_dev // 2 :] + order[: n_dev // 2]]
    exchange = functools.partial(
        lax.all_to_all,
        axis_name=("role", "dev"),
        split_axis=0,
        concat_axis=0,
        axis_index_groups=[orders[0], [n_dev + dev for dev in orders[1]]],
        tiled=True,
    )
    span = n_dev // len(flips)
    wanted = np.zeros((2, len(flips), n_dev, n_dev), np.float32)
    for r in range(2):
        for place, dev in enumerate(orders[r]):
            for i, flip in enumerate(flips):
                wanted[r, place // span, place % span * len(flips) + i, dev ^ flip] = 1.0
    places = np.stack(
        [
            np.stack([np.repeat(each, capacity), np.tile(np.arange(capacity), n_dev)])
            for each in orders
        ]
    )
    steps = [[(dev, dev ^ flip) for dev in range(n_dev)] for flip in flips[1:]]
    other_outs = [lax.ppermute(w_out[0], "dev", step) for step in steps]
    sent, own_lift, own_out, own_resid, taken, combine_weights = attend(
        role_index,
        lengths,
        query,
        cache,
        jnp.asarray(wanted, bf16),
        w_uv[:, 0],
        w_out[0],
        resid,
        expert_ids,
        gate_scores,
        jnp.asarray(places, jnp.int32),
    )
    other_lifts = [lax.ppermute(own_lift, "dev", step) for step in steps]
    gathered = exchange(sent.reshape(n_dev, -1, sent.shape[1]))
    gathered, other_outs, other_lifts, gain = lax.optimization_barrier(
        (gathered, other_outs, other_lifts, norm_gain.reshape(2, half_width))
    )
    own_values = lift_values(gathered.reshape(sent.shape), [own_lift, *other_lifts])
    other_values = lax.ppermute(own_values, "role", swap)
    partial = project(role_index, own_values, other_values, [own_out, *other_outs])
    pieces = exchange(partial)
    hidden, packed = settle(role_index, pieces, own_resid, taken, capacity)
    arrived = exchange(packed)

    outward, own_sums, square_terms = lift_rows(role_index, arrived, gain, w_gate[0], w_up[0])
    inward = lax.ppermute(outward, "role", swap)
    produced = lower_rows(role_index, width, own_sums, inward, square_terms, w_down[0], capacity)
    returned = exchange(produced)

    return combine(combine_weights, returned, hidden)


def solution(mesh):
    return jax.shard_map(
        local,
        mesh=mesh,
        in_specs=(
            P("dev", None),
            P("dev", None, None),
            P("dev", None, None),
            P("dev"),
            P(None, "dev", None),
            P("dev", None, "role"),
            P(),
            P("dev", None),
            P("dev", None),
            P("dev", None, None),
            P("dev", None, None),
            P("dev", None, None),
        ),
        out_specs=P("dev", "role"),
        check_vma=False,
    )
```
